32 devices in a mesh: groups: 2 (over y), ctx: 8 (over z, x), tp: 2 (over core).
Axes of the slice: x: 2, y: 2, z: 4, core: 2. Of those that a mesh axis runs over, the one named last changes fastest.
Arguments:
- queries: bfloat16 [256, 64, 192], P(('groups', 'ctx'), 'tp'), parts along dimension 0, may hold values from -30 to 30
- latent_cache: bfloat16 [4096, 576], P(('groups', 'ctx')), parts along dimension 0, may hold values from -6 to 6
- kv_weight: bfloat16 [512, 64, 256], P('ctx', 'tp'), may hold values from -0.25 to 0.25
- block_order: int32 [16], P('groups'), parts along dimension 0, may hold values from 0 to 7, as said below
- span_start: int32 [2], P('groups'), parts along dimension 0, may hold values from 1024 to 1920
Outputs:
- attended: bfloat16 [256, 64, 128], P(('groups', 'ctx'), 'tp'), parts along dimension 0
The draws below stay inside these ranges and needn't reach their ends.
There are 2 independent parts, one for each index of `groups`. The reference program is written for one: setup_inputs(seed, part) draws one part's arguments, and reference() takes and returns one part's arrays. A program takes and returns all parts, laid end to end along the dimension named above; an argument that names none is the same for every part. Nothing has to cross between parts.
Inputs may be any that keep to these rules, and one draw needn't show every extreme that they name: `block_order`: A permutation: every block of the prompt is stored by exactly one shard.
All inputs are finite; a program needn't handle non-finite values.
Results may differ from the reference program's by a relative error of at most 0.015.
Values may be sent and summed in bfloat16 or wider, within the bound.
No kernel may reach another device: no remote copies, remote signals or barrier semaphores. Data moves between devices by JAX's collectives and lax.ppermute only.
A program may use at most 64 MiB of HBM per device.

```python
import math
import jax
import jax.numpy as jnp
from jax import lax

LAT = 512
ROPE = 64
NOPE = 128
VD = 128
HEADS = 64
Q = 128
CTX_DEV = 256
N_CTX = 8


def shared_order(key):
    return jax.random.permutation(jax.random.fold_in(key, 11), N_CTX).astype(jnp.int32)


def shared_anchor(key):
    sign_bits = jax.random.bernoulli(jax.random.fold_in(key, 12), 0.5, (ROPE,))
    return jnp.where(sign_bits, 2.0, -2.0).astype(jnp.float32)


def draw_block_order(key, part):
    return shared_order(key)


def draw_latent_cache(key, part):
    block_perm = shared_order(key)
    anchor = shared_anchor(key)
    key = jax.random.fold_in(key, 2)
    key_latent, key_rope = jax.random.split(key, 2)
    total_rows = CTX_DEV * N_CTX
    latent = jnp.clip(jax.random.normal(key_latent, (total_rows, LAT), jnp.float32), -4.0, 4.0)
    rope_part = jnp.clip(jax.random.normal(key_rope, (total_rows, ROPE), jnp.float32), -3.0, 3.0)
    first_row = (jnp.argmax(block_perm == 0).astype(jnp.int32) * CTX_DEV).astype(jnp.int32)
    rope_part = rope_part.at[first_row].set(anchor)
    return jnp.concatenate([latent, rope_part], axis=1).astype(jnp.bfloat16)


def draw_queries(key, part):
    key = jax.random.fold_in(key, 3)
    draws = jnp.clip(jax.random.normal(key, (Q, HEADS, NOPE + ROPE), jnp.float32), -4.0, 4.0)
    return draws.astype(jnp.bfloat16)


def shard_levels(own_key, dims, cuts, smallest, top_value):
    loudness, own = 1.0, jax.random.fold_in(own_key, 6)
    for axis_at, shards_of in cuts:
        steps = jnp.exp(jax.random.uniform(jax.random.fold_in(own, axis_at), (shards_of,), jnp.float32, smallest / len(cuts), top_value / len(cuts)))
        loudness = loudness * jnp.repeat(steps, dims[axis_at] // shards_of).reshape([-1 if axis == axis_at else 1 for axis in range(len(dims))])
    return loudness


def gaussian(rng, extent, width, limit, pieces=(), held_as=jnp.bfloat16):
    values = jax.random.normal(rng, extent, jnp.float32) * width
    if len(pieces) > 0:
        values = shard_levels(rng, extent, pieces, -0.22, 0.18) * values
    return jnp.clip(values, min=-limit, max=limit).astype(held_as)


def setup_inputs(seed: int = 0, part: int = 0) -> dict:
    arg_keys = jax.random.split(jax.random.key(seed), 6)
    own_keys = jax.random.split(jax.random.fold_in(arg_keys[5], part), 6)
    return {
        "queries": draw_queries(jax.random.fold_in(jax.random.fold_in(arg_keys[5], part), 71), part),
        "latent_cache": draw_latent_cache(jax.random.fold_in(jax.random.fold_in(arg_keys[5], part), 71), part),
        "kv_weight": gaussian(arg_keys[2], (LAT, HEADS, NOPE + VD), LAT ** -0.5, 0.25, ((0, 8), (1, 2))),
        "block_order": draw_block_order(jax.random.fold_in(jax.random.fold_in(arg_keys[5], part), 71), part),
        "span_start": jax.random.randint(own_keys[4], (1,), CTX_DEV * N_CTX // 2, CTX_DEV * N_CTX - Q + 1).astype(jnp.int32),
    }


def reference(queries, latent_cache, kv_weight, block_order, span_start):
    softmax_scale = 1.0 / math.sqrt(NOPE + ROPE)
    block_rank = jnp.argsort(block_order).astype(jnp.int32)
    ordered = jnp.take(latent_cache.reshape(N_CTX, CTX_DEV, LAT + ROPE), block_rank, axis=0)
    ordered = ordered.reshape(N_CTX * CTX_DEV, LAT + ROPE)
    latent = ordered[:, :LAT]
    rope_keys = ordered[:, LAT:]
    positions = jnp.arange(N_CTX * CTX_DEV, dtype=jnp.int32)
    query_last = span_start[0] + jnp.arange(Q, dtype=jnp.int32)
    visible = positions[None, :] <= query_last[:, None]

    def one_head(head):
        head_weight = lax.dynamic_index_in_dim(kv_weight, head, 1, keepdims=False)
        key_value = jnp.dot(latent, head_weight, preferred_element_type=jnp.float32).astype(jnp.bfloat16)
        head_keys = jnp.concatenate([key_value[:, :NOPE], rope_keys], axis=1)
        head_query = lax.dynamic_index_in_dim(queries, head, 1, keepdims=False)
        scores = jnp.dot(head_query, head_keys.T, preferred_element_type=jnp.float32) * softmax_scale
        scores = jnp.where(visible, scores, jnp.float32(-1e+30))
        row_max = lax.optimization_barrier(jnp.max(scores, axis=1, keepdims=True))
        weights = jnp.where(visible, jnp.exp(scores - row_max), jnp.float32(0.0))
        row_total = lax.optimization_barrier(jnp.sum(weights, axis=1, keepdims=True))
        result = jnp.dot(weights.astype(jnp.bfloat16), key_value[:, NOPE:], preferred_element_type=jnp.float32) / row_total
        return result.astype(jnp.bfloat16)
    outputs = lax.map(one_head, jnp.arange(HEADS, dtype=jnp.int32))
    return jnp.transpose(outputs, (1, 0, 2))
```

```python
import functools
import math

import jax
import jax.numpy as jnp
from jax import lax
from jax.experimental import pallas as pl
from jax.experimental.pallas import tpu as pltpu
from jax.sharding import PartitionSpec as P

LAT = 512
ROPE = 64
NOPE = 128
VD = 128
HIDDEN = -1e30


def attend_kernel(
    slots, rows, halves, heads,
    order_ref, start_ref, weight_ref, query_ref, *refs,
):
    piece_refs = refs[: 1 + 2 * (slots - 1)]
    out_ref, latent, keys, sems = refs[1 + 2 * (slots - 1):]
    half = rows // halves
    me = lax.axis_index("ctx")
    core = lax.axis_index("tp")
    copies = [pltpu.make_async_copy(piece_refs[0], latent.at[pl.ds(0, rows)], sems.at[0])]
    for slot in range(1, slots):
        for which in range(2):
            at = core if which == 0 else 1 - core
            place = pl.multiple_of(slot * rows + at * half, half)
            index = 2 * slot - 1 + which
            copies.append(
                pltpu.make_async_copy(
                    piece_refs[index], latent.at[pl.ds(place, half)], sems.at[index]
                )
            )
    for copy in copies:
        copy.start()
    for copy in copies:
        copy.wait()
    total_rows = slots * rows
    query_count = query_ref.shape[0] * query_ref.shape[1]
    scale = math.log2(math.e) / math.sqrt(NOPE + ROPE)
    rope = latent[:, LAT:]
    tail = jnp.concatenate([rope, jnp.zeros_like(rope)], axis=1)
    for buffer in range(2):
        keys[buffer, :, NOPE:] = tail
    ahead = lax.broadcasted_iota(jnp.int32, (query_count, rows), 1) - lax.broadcasted_iota(
        jnp.int32, (query_count, rows), 0
    )
    limits = [start_ref[0] - order_ref[me ^ slot] * rows for slot in range(slots)]
    for head in range(heads):
        buffer = head % 2
        weight = weight_ref[:, :, head * (NOPE + VD):(head + 1) * (NOPE + VD)]
        weight = weight.reshape(LAT, NOPE + VD)
        key_value = jnp.dot(latent[:, :LAT], weight, preferred_element_type=jnp.float32)
        key_value = key_value.astype(jnp.bfloat16)
        keys[buffer, :, :NOPE] = key_value[:, :NOPE]
        values = key_value[:, NOPE:]
        query = query_ref[:, :, head * 256:(head + 1) * 256].reshape(query_count, 256)
        scores = lax.dot_general(
            query, keys[buffer], (((1,), (1,)), ((), ())), preferred_element_type=jnp.float32
        )
        scores = jnp.concatenate(
            [
                jnp.where(
                    ahead <= limits[slot], scores[:, slot * rows:(slot + 1) * rows], HIDDEN
                )
                for slot in range(slots)
            ],
            axis=1,
        )
        top = jnp.max(scores, axis=1, keepdims=True)
        probs = jnp.exp2((scores - top) * scale)
        totals = jnp.sum(probs, axis=1, keepdims=True)
        result = jnp.dot(probs.astype(jnp.bfloat16), values, preferred_element_type=jnp.float32)
        out_ref[:, head * VD:(head + 1) * VD] = (result / totals).astype(jnp.bfloat16)


def split_by_heads(contexts, cores, queries, latent_cache, kv_weight, block_order, span_start):
    query_rows, head_count, query_width = queries.shape
    heads = head_count // contexts
    rows = latent_cache.shape[0]
    half = rows // cores
    weight_rows = kv_weight.shape[0]

    def swap(array, bit):
        return lax.ppermute(array, "ctx", [(i, i ^ bit) for i in range(contexts)])

    weight = kv_weight.reshape(weight_rows, contexts, heads * (NOPE + VD)).transpose(1, 0, 2)
    padded = jnp.pad(queries, ((0, 0), (0, 0), (0, 256 - query_width)))
    query = padded.reshape(query_rows, contexts, heads * 256).transpose(1, 0, 2)
    packed = jnp.concatenate([weight, query], axis=1)
    packed = lax.all_to_all(packed, "ctx", 0, 0, tiled=True)
    weight = packed[:, :weight_rows]
    query = packed[:, weight_rows:]

    core = lax.axis_index("tp")
    held = {0: lax.dynamic_slice_in_dim(latent_cache, core * half, half, 0)}
    bits = []
    bit = contexts // 2
    while bit >= 1:
        bits.append(bit)
        bit //= 2
    for bit in bits:
        for slot in list(held):
            held[slot | bit] = swap(held[slot], bit)
    pieces = [latent_cache]
    for slot in range(1, contexts):
        pieces.append(held[slot])
        pieces.append(lax.ppermute(held[slot], "tp", [(0, 1), (1, 0)]))

    total_rows = contexts * rows
    query_count = contexts * query_rows
    anywhere = pl.BlockSpec(memory_space=pl.ANY)
    on_chip = pl.BlockSpec(memory_space=pltpu.VMEM)
    scalars = pl.BlockSpec(memory_space=pltpu.SMEM)
    attended = pl.pallas_call(
        functools.partial(attend_kernel, contexts, rows, cores, heads),
        out_shape=jax.ShapeDtypeStruct((query_count, heads * VD), jnp.bfloat16),
        in_specs=[scalars, scalars, on_chip, on_chip] + [anywhere] * len(pieces),
        out_specs=on_chip,
        scratch_shapes=[
            pltpu.VMEM((total_rows, LAT + ROPE), jnp.bfloat16),
            pltpu.VMEM((2, total_rows, 256), jnp.bfloat16),
            pltpu.SemaphoreType.DMA((len(pieces),)),
        ],
        compiler_params=pltpu.CompilerParams(vmem_limit_bytes=48 * 2**20),
        name="attend",
    )(block_order, span_start, weight, query, *pieces)
    attended = attended.reshape(contexts, query_rows, heads * VD)
    attended = lax.all_to_all(attended, "ctx", 0, 0, tiled=True)
    attended = attended.reshape(contexts, query_rows, heads, VD).transpose(1, 0, 2, 3)
    return attended.reshape(query_rows, head_count, VD)


def tile_update(running, tile_rows, tile_positions, gathered_queries, weight_matrix, query_last):
    row_max, row_total, accum = running
    softmax_scale = 1.0 / math.sqrt(NOPE + ROPE)
    head_count = gathered_queries.shape[1]
    latent = tile_rows[:, :LAT]
    rope_part = tile_rows[:, LAT:]
    key_value = jnp.dot(latent, weight_matrix, preferred_element_type=jnp.float32).astype(
        jnp.bfloat16
    )
    key_value = key_value.reshape(tile_rows.shape[0], head_count, NOPE + VD)
    scores = jnp.einsum(
        "qhc,khc->hqk",
        gathered_queries[:, :, :NOPE],
        key_value[:, :, :NOPE],
        preferred_element_type=jnp.float32,
    )
    scores = scores + jnp.einsum(
        "qhr,kr->hqk", gathered_queries[:, :, NOPE:], rope_part, preferred_element_type=jnp.float32
    )
    scores = scores * softmax_scale
    visible = (tile_positions[None, :] <= query_last[:, None])[None]
    scores = jnp.where(visible, scores, jnp.float32(-1e30))
    new_max = jnp.maximum(row_max, jnp.max(scores, axis=2))
    weights = jnp.where(visible, jnp.exp(scores - new_max[:, :, None]), jnp.float32(0.0))
    row_total = jnp.sum(weights, axis=2)
    accum = jnp.einsum(
        "hqk,khv->hqv",
        weights.astype(jnp.bfloat16),
        key_value[:, :, NOPE:],
        preferred_element_type=jnp.float32,
    )
    return (new_max, row_total, accum)


def split_by_context(queries, latent_cache, kv_weight, block_order, span_start):
    shard_index = lax.axis_index("ctx")
    gathered_queries = lax.all_gather(queries, "ctx", axis=0, tiled=True)
    full_weight = lax.all_gather(kv_weight, "ctx", axis=0, tiled=True)
    head_count = full_weight.shape[1]
    weight_matrix = full_weight.reshape(LAT, head_count * (NOPE + VD))
    row_count = latent_cache.shape[0]
    own_block = lax.dynamic_index_in_dim(block_order, shard_index, 0, keepdims=False)
    key_positions = own_block * row_count + jnp.arange(row_count, dtype=jnp.int32)
    query_count = gathered_queries.shape[0]
    query_last = span_start[0] + jnp.arange(query_count, dtype=jnp.int32)
    final_position = span_start[0] + query_count - 1
    running = (
        jnp.full((head_count, query_count), -1e30, jnp.float32),
        jnp.zeros((head_count, query_count), jnp.float32),
        jnp.zeros((head_count, query_count, VD), jnp.float32),
    )
    running = lax.cond(
        key_positions[0] <= final_position,
        lambda current, rows_now=latent_cache, places=key_positions: tile_update(
            current, rows_now, places, gathered_queries, weight_matrix, query_last
        ),
        lambda current: current,
        running,
    )
    row_max, row_total, accum = running
    parts_accum, parts_max, parts_total = (
        lax.all_to_all(
            accum[:, :, None, :].astype(jnp.bfloat16),
            "ctx",
            split_axis=1,
            concat_axis=2,
            tiled=True,
        ).astype(jnp.float32),
        lax.all_to_all(
            row_max[:, :, None].astype(jnp.bfloat16), "ctx", split_axis=1, concat_axis=2, tiled=True
        ).astype(jnp.float32),
        lax.all_to_all(
            row_total[:, :, None].astype(jnp.bfloat16),
            "ctx",
            split_axis=1,
            concat_axis=2,
            tiled=True,
        ).astype(jnp.float32),
    )
    overall = jnp.max(parts_max, axis=2, keepdims=True)
    factor = jnp.exp(parts_max - overall)
    denominator = jnp.sum(factor * parts_total, axis=2)
    numerator = jnp.sum(factor[:, :, :, None] * parts_accum, axis=2)
    result = (numerator / denominator[:, :, None]).astype(jnp.bfloat16)
    return jnp.transpose(result, (1, 0, 2))


def solution(mesh):
    contexts = mesh.shape["ctx"]
    cores = mesh.shape["tp"]

    def local(queries, latent_cache, kv_weight, block_order, span_start):
        arrays = (queries, latent_cache, kv_weight, block_order, span_start)
        whole_heads = queries.shape[1] % contexts == 0 and contexts & (contexts - 1) == 0
        if whole_heads and cores == 2:
            return split_by_heads(contexts, cores, *arrays)
        return split_by_context(*arrays)

    return jax.shard_map(
        local,
        mesh=mesh,
        in_specs=(
            P(("groups", "ctx"), "tp", None),
            P(("groups", "ctx"), None),
            P("ctx", "tp", None),
            P("groups"),
            P("groups"),
        ),
        out_specs=P(("groups", "ctx"), "tp", None),
        check_vma=False,
    )
```

```python
import functools
import math

import jax
import jax.numpy as jnp
from jax import lax
from jax.experimental import pallas as pl
from jax.experimental.pallas import tpu as pltpu
from jax.sharding import PartitionSpec as P

LAT = 512
ROPE = 64
NOPE = 128
VD = 128
HIDDEN = -1e30
ROUNDS = ((4, 0, 4), (2, 0, 2), (1, 0, 1), (3, 2, 1), (5, 4, 1), (6, 4, 2), (7, 5, 2))


def attend_kernel(slots, rows, halves, pair, *refs):
    order_ref, start_ref, packed_ref, other_ref = refs[:4]
    piece_refs = refs[4: 5 + 2 * (slots - 1)]
    out_ref, latent, keys, sems = refs[5 + 2 * (slots - 1):]
    half = rows // halves
    me = lax.axis_index("ctx")
    core = lax.axis_index("tp")
    copies = [pltpu.make_async_copy(piece_refs[0], latent.at[pl.ds(0, rows)], sems.at[0])]
    for slot in range(1, slots):
        for which in range(2):
            at = core if which == 0 else 1 - core
            place = pl.multiple_of(slot * rows + at * half, half)
            index = 2 * slot - 1 + which
            copies.append(
                pltpu.make_async_copy(
                    piece_refs[index], latent.at[pl.ds(place, half)], sems.at[index]
                )
            )
    for copy in copies:
        copy.start()
    for copy in copies:
        copy.wait()
    width = NOPE + VD
    depth = other_ref.shape[1] // pair
    query_rows = (packed_ref.shape[1] - pair * depth) // 3
    query_count = slots * query_rows
    scale = math.log2(math.e) / math.sqrt(NOPE + ROPE)
    rope = latent[:, LAT:]
    tail = jnp.concatenate([rope, jnp.zeros_like(rope)], axis=1)
    for buffer in range(2):
        keys[buffer, :, NOPE:] = tail
    ahead = lax.broadcasted_iota(jnp.int32, (query_count, rows), 1) - lax.broadcasted_iota(
        jnp.int32, (query_count, rows), 0
    )
    limits = [start_ref[0] - order_ref[me ^ slot] * rows for slot in range(slots)]
    first = pair * depth
    for head in range(2 * pair):
        buffer = head % 2
        which, member = divmod(head, pair)
        weight_ref = packed_ref if which == 0 else other_ref
        weight = weight_ref[:, member * depth:(member + 1) * depth, :].reshape(LAT, width)
        key_value = jnp.dot(latent[:, :LAT], weight, preferred_element_type=jnp.float32)
        key_value = key_value.astype(jnp.bfloat16)
        keys[buffer, :, :NOPE] = key_value[:, :NOPE]
        values = key_value[:, NOPE:]
        begin = first + which * query_rows
        part = packed_ref[:, begin:begin + query_rows, member * NOPE:(member + 1) * NOPE]
        part = part.reshape(query_count, NOPE)
        begin = first + 2 * query_rows
        turned = packed_ref[:, begin:begin + query_rows, head * ROPE:(head + 1) * ROPE]
        turned = turned.reshape(query_count, ROPE)
        query = jnp.concatenate([part, turned, jnp.zeros_like(turned)], axis=1)
        scores = lax.dot_general(
            query, keys[buffer], (((1,), (1,)), ((), ())), preferred_element_type=jnp.float32
        )
        scores = jnp.concatenate(
            [
                jnp.where(
                    ahead <= limits[slot], scores[:, slot * rows:(slot + 1) * rows], HIDDEN
                )
                for slot in range(slots)
            ],
            axis=1,
        )
        top = jnp.max(scores, axis=1, keepdims=True)
        probs = jnp.exp2((scores - top) * scale)
        totals = jnp.sum(probs, axis=1, keepdims=True)
        result = jnp.dot(probs.astype(jnp.bfloat16), values, preferred_element_type=jnp.float32)
        out_ref[:, head * VD:(head + 1) * VD] = (result / totals).astype(jnp.bfloat16)


def split_by_heads(contexts, cores, queries, latent_cache, kv_weight, block_order, span_start):
    query_rows, head_count, query_width = queries.shape
    heads = head_count // contexts
    pair = heads // 2
    rows = latent_cache.shape[0]
    half = rows // cores
    depth = kv_weight.shape[0]
    width = NOPE + VD
    group = lax.axis_index("groups")

    def swap(array, bit):
        return lax.ppermute(array, "ctx", [(i, i ^ bit) for i in range(contexts)])

    weight = kv_weight.reshape(depth, contexts, 2, pair, width)
    weight = lax.dynamic_index_in_dim(weight, group, 2, keepdims=False)
    weight = weight.transpose(1, 2, 0, 3).reshape(contexts, pair * depth, width)
    query = queries.reshape(query_rows, contexts, 2, pair, query_width)
    query = jnp.where(group == 0, query, query[:, :, ::-1])
    straight = query[..., :NOPE].transpose(1, 2, 0, 3, 4)
    straight = straight.reshape(contexts, 2 * query_rows, pair * NOPE)
    turned = query[..., NOPE:].transpose(1, 0, 2, 3, 4)
    turned = turned.reshape(contexts, query_rows, heads * ROPE)
    packed = jnp.concatenate([weight, straight, turned], axis=1)
    packed = lax.all_to_all(packed, "ctx", 0, 0, tiled=True)
    other = lax.ppermute(packed[:, :pair * depth], "groups", [(0, 1), (1, 0)])

    core = lax.axis_index("tp")
    held = {0: lax.dynamic_slice_in_dim(latent_cache, core * half, half, 0)}
    for slot, source, bit in ROUNDS:
        held[slot] = swap(held[source], bit)
    pieces = [latent_cache]
    for slot in range(1, contexts):
        pieces.append(held[slot])
        pieces.append(lax.ppermute(held[slot], "tp", [(0, 1), (1, 0)]))

    total_rows = contexts * rows
    query_count = contexts * query_rows
    anywhere = pl.BlockSpec(memory_space=pl.ANY)
    on_chip = pl.BlockSpec(memory_space=pltpu.VMEM)
    scalars = pl.BlockSpec(memory_space=pltpu.SMEM)
    attended = pl.pallas_call(
        functools.partial(attend_kernel, contexts, rows, cores, pair),
        out_shape=jax.ShapeDtypeStruct((query_count, heads * VD), jnp.bfloat16),
        in_specs=[scalars, scalars, on_chip, on_chip] + [anywhere] * len(pieces),
        out_specs=on_chip,
        scratch_shapes=[
            pltpu.VMEM((total_rows, LAT + ROPE), jnp.bfloat16),
            pltpu.VMEM((2, total_rows, 256), jnp.bfloat16),
            pltpu.SemaphoreType.DMA((len(pieces),)),
        ],
        compiler_params=pltpu.CompilerParams(vmem_limit_bytes=48 * 2**20),
        name="attend",
    )(block_order, span_start, packed, other, *pieces)
    attended = attended.reshape(contexts, query_rows, heads * VD)
    attended = lax.all_to_all(attended, "ctx", 0, 0, tiled=True)
    attended = attended.reshape(contexts, query_rows, 2, pair, VD)
    attended = jnp.where(group == 0, attended, attended[:, :, ::-1])
    attended = attended.transpose(1, 0, 2, 3, 4)
    return attended.reshape(query_rows, head_count, VD)


def tile_update(running, tile_rows, tile_positions, gathered_queries, weight_matrix, query_last):
    row_max, row_total, accum = running
    softmax_scale = 1.0 / math.sqrt(NOPE + ROPE)
    head_count = gathered_queries.shape[1]
    latent = tile_rows[:, :LAT]
    rope_part = tile_rows[:, LAT:]
    key_value = jnp.dot(latent, weight_matrix, preferred_element_type=jnp.float32).astype(
        jnp.bfloat16
    )
    key_value = key_value.reshape(tile_rows.shape[0], head_count, NOPE + VD)
    scores = jnp.einsum(
        "qhc,khc->hqk",
        gathered_queries[:, :, :NOPE],
        key_value[:, :, :NOPE],
        preferred_element_type=jnp.float32,
    )
    scores = scores + jnp.einsum(
        "qhr,kr->hqk", gathered_queries[:, :, NOPE:], rope_part, preferred_element_type=jnp.float32
    )
    scores = scores * softmax_scale
    visible = (tile_positions[None, :] <= query_last[:, None])[None]
    scores = jnp.where(visible, scores, jnp.float32(-1e30))
    new_max = jnp.maximum(row_max, jnp.max(scores, axis=2))
    weights = jnp.where(visible, jnp.exp(scores - new_max[:, :, None]), jnp.float32(0.0))
    row_total = jnp.sum(weights, axis=2)
    accum = jnp.einsum(
        "hqk,khv->hqv",
        weights.astype(jnp.bfloat16),
        key_value[:, :, NOPE:],
        preferred_element_type=jnp.float32,
    )
    return (new_max, row_total, accum)


def split_by_context(queries, latent_cache, kv_weight, block_order, span_start):
    shard_index = lax.axis_index("ctx")
    gathered_queries = lax.all_gather(queries, "ctx", axis=0, tiled=True)
    full_weight = lax.all_gather(kv_weight, "ctx", axis=0, tiled=True)
    head_count = full_weight.shape[1]
    weight_matrix = full_weight.reshape(LAT, head_count * (NOPE + VD))
    row_count = latent_cache.shape[0]
    own_block = lax.dynamic_index_in_dim(block_order, shard_index, 0, keepdims=False)
    key_positions = own_block * row_count + jnp.arange(row_count, dtype=jnp.int32)
    query_count = gathered_queries.shape[0]
    query_last = span_start[0] + jnp.arange(query_count, dtype=jnp.int32)
    final_position = span_start[0] + query_count - 1
    running = (
        jnp.full((head_count, query_count), -1e30, jnp.float32),
        jnp.zeros((head_count, query_count), jnp.float32),
        jnp.zeros((head_count, query_count, VD), jnp.float32),
    )
    running = lax.cond(
        key_positions[0] <= final_position,
        lambda current, rows_now=latent_cache, places=key_positions: tile_update(
            current, rows_now, places, gathered_queries, weight_matrix, query_last
        ),
        lambda current: current,
        running,
    )
    row_max, row_total, accum = running
    parts_accum, parts_max, parts_total = (
        lax.all_to_all(
            accum[:, :, None, :].astype(jnp.bfloat16),
            "ctx",
            split_axis=1,
            concat_axis=2,
            tiled=True,
        ).astype(jnp.float32),
        lax.all_to_all(
            row_max[:, :, None].astype(jnp.bfloat16), "ctx", split_axis=1, concat_axis=2, tiled=True
        ).astype(jnp.float32),
        lax.all_to_all(
            row_total[:, :, None].astype(jnp.bfloat16),
            "ctx",
            split_axis=1,
            concat_axis=2,
            tiled=True,
        ).astype(jnp.float32),
    )
    overall = jnp.max(parts_max, axis=2, keepdims=True)
    factor = jnp.exp(parts_max - overall)
    denominator = jnp.sum(factor * parts_total, axis=2)
    numerator = jnp.sum(factor[:, :, :, None] * parts_accum, axis=2)
    result = (numerator / denominator[:, :, None]).astype(jnp.bfloat16)
    return jnp.transpose(result, (1, 0, 2))


def solution(mesh):
    contexts = mesh.shape["ctx"]
    cores = mesh.shape["tp"]

    def local(queries, latent_cache, kv_weight, block_order, span_start):
        arrays = (queries, latent_cache, kv_weight, block_order, span_start)
        paired = queries.shape[1] % (2 * contexts) == 0 and contexts == len(ROUNDS) + 1
        if paired and cores == 2 and mesh.shape["groups"] == 2:
            return split_by_heads(contexts, cores, *arrays)
        return split_by_context(*arrays)

    return jax.shard_map(
        local,
        mesh=mesh,
        in_specs=(
            P(("groups", "ctx"), "tp", None),
            P(("groups", "ctx"), None),
            P("ctx", "tp", None),
            P("groups"),
            P("groups"),
        ),
        out_specs=P(("groups", "ctx"), "tp", None),
        check_vma=False,
    )
```

```python
import functools
import math

import jax
import jax.numpy as jnp
from jax import lax
from jax.experimental import pallas as pl
from jax.experimental.pallas import tpu as pltpu
from jax.sharding import PartitionSpec as P

LAT = 512
ROPE = 64
NOPE = 128
VD = 128
HIDDEN = -1e30
EARLY = ((4, 0, 4), (2, 0, 2), (1, 0, 1), (3, 0, 3))
LATE = ((5, 4, 1), (6, 4, 2), (7, 4, 3))


def attend_kernel(slots, rows, halves, pair, *refs):
    order_ref, start_ref, packed_ref, other_ref = refs[:4]
    piece_refs = refs[4: 5 + 2 * (slots - 1)]
    out_ref, latent, keys, sems = refs[5 + 2 * (slots - 1):]
    half = rows // halves
    me = lax.axis_index("ctx")
    core = lax.axis_index("tp")
    copies = [pltpu.make_async_copy(piece_refs[0], latent.at[pl.ds(0, rows)], sems.at[0])]
    for slot in range(1, slots):
        for which in range(2):
            at = core if which == 0 else 1 - core
            place = pl.multiple_of(slot * rows + at * half, half)
            index = 2 * slot - 1 + which
            copies.append(
                pltpu.make_async_copy(
                    piece_refs[index], latent.at[pl.ds(place, half)], sems.at[index]
                )
            )
    for copy in copies:
        copy.start()
    for copy in copies:
        copy.wait()
    width = NOPE + VD
    depth = other_ref.shape[1] // pair
    query_rows = (packed_ref.shape[1] - pair * depth) // 3
    query_count = slots * query_rows
    scale = math.log2(math.e) / math.sqrt(NOPE + ROPE)
    rope = latent[:, LAT:]
    tail = jnp.concatenate([rope, jnp.zeros_like(rope)], axis=1)
    for buffer in range(2):
        keys[buffer, :, NOPE:] = tail
    ahead = lax.broadcasted_iota(jnp.int32, (query_count, rows), 1) - lax.broadcasted_iota(
        jnp.int32, (query_count, rows), 0
    )
    limits = [start_ref[0] - order_ref[me ^ slot] * rows for slot in range(slots)]
    first = pair * depth
    for head in range(2 * pair):
        buffer = head % 2
        which, member = divmod(head, pair)
        weight_ref = packed_ref if which == 0 else other_ref
        weight = weight_ref[:, member * depth:(member + 1) * depth, :].reshape(LAT, width)
        key_value = jnp.dot(latent[:, :LAT], weight, preferred_element_type=jnp.float32)
        key_value = key_value.astype(jnp.bfloat16)
        keys[buffer, :, :NOPE] = key_value[:, :NOPE]
        values = key_value[:, NOPE:]
        begin = first + which * query_rows
        part = packed_ref[:, begin:begin + query_rows, member * NOPE:(member + 1) * NOPE]
        part = part.reshape(query_count, NOPE)
        begin = first + 2 * query_rows
        turned = packed_ref[:, begin:begin + query_rows, head * ROPE:(head + 1) * ROPE]
        turned = turned.reshape(query_count, ROPE)
        query = jnp.concatenate([part, turned, jnp.zeros_like(turned)], axis=1)
        scores = lax.dot_general(
            query, keys[buffer], (((1,), (1,)), ((), ())), preferred_element_type=jnp.float32
        )
        scores = jnp.concatenate(
            [
                jnp.where(
                    ahead <= limits[slot], scores[:, slot * rows:(slot + 1) * rows], HIDDEN
                )
                for slot in range(slots)
            ],
            axis=1,
        )
        top = jnp.max(scores, axis=1, keepdims=True)
        probs = jnp.exp2((scores - top) * scale)
        totals = jnp.sum(probs, axis=1, keepdims=True)
        result = jnp.dot(probs.astype(jnp.bfloat16), values, preferred_element_type=jnp.float32)
        out_ref[:, head * VD:(head + 1) * VD] = (result / totals).astype(jnp.bfloat16)


def split_by_heads(contexts, cores, queries, latent_cache, kv_weight, block_order, span_start):
    query_rows, head_count, query_width = queries.shape
    heads = head_count // contexts
    pair = heads // 2
    rows = latent_cache.shape[0]
    half = rows // cores
    depth = kv_weight.shape[0]
    width = NOPE + VD
    group = lax.axis_index("groups")

    def swap(array, bit):
        return lax.ppermute(array, "ctx", [(i, i ^ bit) for i in range(contexts)])

    weight = kv_weight.reshape(depth, contexts, 2, pair, width)
    weight = lax.dynamic_index_in_dim(weight, group, 2, keepdims=False)
    weight = weight.transpose(1, 2, 0, 3).reshape(contexts, pair * depth, width)
    query = queries.reshape(query_rows, contexts, 2, pair, query_width)
    query = jnp.where(group == 0, query, query[:, :, ::-1])
    straight = query[..., :NOPE].transpose(1, 2, 0, 3, 4)
    straight = straight.reshape(contexts, 2 * query_rows, pair * NOPE)
    turned = query[..., NOPE:].transpose(1, 0, 2, 3, 4)
    turned = turned.reshape(contexts, query_rows, heads * ROPE)
    packed = jnp.concatenate([weight, straight, turned], axis=1)
    packed = lax.all_to_all(packed, "ctx", 0, 0, tiled=True)
    core = lax.axis_index("tp")
    held = {0: lax.dynamic_slice_in_dim(latent_cache, core * half, half, 0)}
    for slot, source, bit in EARLY:
        held[slot] = swap(held[source], bit)
    waited = lax.optimization_barrier((packed, held[1], held[2], held[3]))
    packed, held[1], held[2], held[3] = waited
    other = lax.ppermute(packed[:, :pair * depth], "groups", [(0, 1), (1, 0)])
    for slot, source, bit in LATE:
        held[slot] = swap(held[source], bit)
    pieces = [latent_cache]
    for slot in range(1, contexts):
        pieces.append(held[slot])
        pieces.append(lax.ppermute(held[slot], "tp", [(0, 1), (1, 0)]))

    total_rows = contexts * rows
    query_count = contexts * query_rows
    anywhere = pl.BlockSpec(memory_space=pl.ANY)
    on_chip = pl.BlockSpec(memory_space=pltpu.VMEM)
    scalars = pl.BlockSpec(memory_space=pltpu.SMEM)
    attended = pl.pallas_call(
        functools.partial(attend_kernel, contexts, rows, cores, pair),
        out_shape=jax.ShapeDtypeStruct((query_count, heads * VD), jnp.bfloat16),
        in_specs=[scalars, scalars, on_chip, on_chip] + [anywhere] * len(pieces),
        out_specs=on_chip,
        scratch_shapes=[
            pltpu.VMEM((total_rows, LAT + ROPE), jnp.bfloat16),
            pltpu.VMEM((2, total_rows, 256), jnp.bfloat16),
            pltpu.SemaphoreType.DMA((len(pieces),)),
        ],
        compiler_params=pltpu.CompilerParams(vmem_limit_bytes=48 * 2**20),
        name="attend",
    )(block_order, span_start, packed, other, *pieces)
    attended = attended.reshape(contexts, query_rows, heads * VD)
    attended = lax.all_to_all(attended, "ctx", 0, 0, tiled=True)
    attended = attended.reshape(contexts, query_rows, 2, pair, VD)
    attended = jnp.where(group == 0, attended, attended[:, :, ::-1])
    attended = attended.transpose(1, 0, 2, 3, 4)
    return attended.reshape(query_rows, head_count, VD)


def tile_update(running, tile_rows, tile_positions, gathered_queries, weight_matrix, query_last):
    row_max, row_total, accum = running
    softmax_scale = 1.0 / math.sqrt(NOPE + ROPE)
    head_count = gathered_queries.shape[1]
    latent = tile_rows[:, :LAT]
    rope_part = tile_rows[:, LAT:]
    key_value = jnp.dot(latent, weight_matrix, preferred_element_type=jnp.float32).astype(
        jnp.bfloat16
    )
    key_value = key_value.reshape(tile_rows.shape[0], head_count, NOPE + VD)
    scores = jnp.einsum(
        "qhc,khc->hqk",
        gathered_queries[:, :, :NOPE],
        key_value[:, :, :NOPE],
        preferred_element_type=jnp.float32,
    )
    scores = scores + jnp.einsum(
        "qhr,kr->hqk", gathered_queries[:, :, NOPE:], rope_part, preferred_element_type=jnp.float32
    )
    scores = scores * softmax_scale
    visible = (tile_positions[None, :] <= query_last[:, None])[None]
    scores = jnp.where(visible, scores, jnp.float32(-1e30))
    new_max = jnp.maximum(row_max, jnp.max(scores, axis=2))
    weights = jnp.where(visible, jnp.exp(scores - new_max[:, :, None]), jnp.float32(0.0))
    row_total = jnp.sum(weights, axis=2)
    accum = jnp.einsum(
        "hqk,khv->hqv",
        weights.astype(jnp.bfloat16),
        key_value[:, :, NOPE:],
        preferred_element_type=jnp.float32,
    )
    return (new_max, row_total, accum)


def split_by_context(queries, latent_cache, kv_weight, block_order, span_start):
    shard_index = lax.axis_index("ctx")
    gathered_queries = lax.all_gather(queries, "ctx", axis=0, tiled=True)
    full_weight = lax.all_gather(kv_weight, "ctx", axis=0, tiled=True)
    head_count = full_weight.shape[1]
    weight_matrix = full_weight.reshape(LAT, head_count * (NOPE + VD))
    row_count = latent_cache.shape[0]
    own_block = lax.dynamic_index_in_dim(block_order, shard_index, 0, keepdims=False)
    key_positions = own_block * row_count + jnp.arange(row_count, dtype=jnp.int32)
    query_count = gathered_queries.shape[0]
    query_last = span_start[0] + jnp.arange(query_count, dtype=jnp.int32)
    final_position = span_start[0] + query_count - 1
    running = (
        jnp.full((head_count, query_count), -1e30, jnp.float32),
        jnp.zeros((head_count, query_count), jnp.float32),
        jnp.zeros((head_count, query_count, VD), jnp.float32),
    )
    running = lax.cond(
        key_positions[0] <= final_position,
        lambda current, rows_now=latent_cache, places=key_positions: tile_update(
            current, rows_now, places, gathered_queries, weight_matrix, query_last
        ),
        lambda current: current,
        running,
    )
    row_max, row_total, accum = running
    parts_accum, parts_max, parts_total = (
        lax.all_to_all(
            accum[:, :, None, :].astype(jnp.bfloat16),
            "ctx",
            split_axis=1,
            concat_axis=2,
            tiled=True,
        ).astype(jnp.float32),
        lax.all_to_all(
            row_max[:, :, None].astype(jnp.bfloat16), "ctx", split_axis=1, concat_axis=2, tiled=True
        ).astype(jnp.float32),
        lax.all_to_all(
            row_total[:, :, None].astype(jnp.bfloat16),
            "ctx",
            split_axis=1,
            concat_axis=2,
            tiled=True,
        ).astype(jnp.float32),
    )
    overall = jnp.max(parts_max, axis=2, keepdims=True)
    factor = jnp.exp(parts_max - overall)
    denominator = jnp.sum(factor * parts_total, axis=2)
    numerator = jnp.sum(factor[:, :, :, None] * parts_accum, axis=2)
    result = (numerator / denominator[:, :, None]).astype(jnp.bfloat16)
    return jnp.transpose(result, (1, 0, 2))


def solution(mesh):
    contexts = mesh.shape["ctx"]
    cores = mesh.shape["tp"]

    def local(queries, latent_cache, kv_weight, block_order, span_start):
        arrays = (queries, latent_cache, kv_weight, block_order, span_start)
        paired = queries.shape[1] % (2 * contexts) == 0 and contexts == 1 + len(EARLY) + len(LATE)
        if paired and cores == 2 and mesh.shape["groups"] == 2:
            return split_by_heads(contexts, cores, *arrays)
        return split_by_context(*arrays)

    return jax.shard_map(
        local,
        mesh=mesh,
        in_specs=(
            P(("groups", "ctx"), "tp", None),
            P(("groups", "ctx"), None),
            P("ctx", "tp", None),
            P("groups"),
            P("groups"),
        ),
        out_specs=P(("groups", "ctx"), "tp", None),
        check_vma=False,
    )
```

```python
import functools
import math

import jax
import jax.numpy as jnp
from jax import lax
from jax.experimental import pallas as pl
from jax.experimental.pallas import tpu as pltpu
from jax.sharding import PartitionSpec as P

LAT = 512
ROPE = 64
NOPE = 128
VD = 128
HIDDEN = -1e30
CHUNK = 512
EARLY = ((4, 0, 4), (1, 0, 1), (2, 0, 2))
LATE = ((3, 2, 1), (5, 4, 1), (6, 4, 2), (7, 5, 2))


def attend_kernel(slots, rows, pair, which, *refs):
    order_ref, start_ref, packed_ref = refs[:3]
    if which == 0:
        weight_ref = packed_ref
        refs = refs[3:]
    else:
        weight_ref, done_ref = refs[3:5]
        refs = refs[5:]
    piece_refs = refs[:5]
    out_ref, latent, keys, values, sems = refs[5:]
    near = slots // 2
    me = lax.axis_index("ctx")
    core = lax.axis_index("tp")
    places = [
        latent.at[0],
        latent.at[pl.ds(1, near - 1), core],
        latent.at[pl.ds(1, near - 1), 1 - core],
        latent.at[pl.ds(near, near), core],
        latent.at[pl.ds(near, near), 1 - core],
    ]
    copies = [
        pltpu.make_async_copy(piece, place, sems.at[index])
        for index, (piece, place) in enumerate(zip(piece_refs, places))
    ]
    for copy in copies:
        copy.start()
    for copy in copies:
        copy.wait()
    width = NOPE + VD
    depth = LAT // slots
    query_rows = (packed_ref.shape[1] - pair * depth) // 3
    query_count = slots * query_rows
    scale = math.log2(math.e) / math.sqrt(NOPE + ROPE)
    rope = latent[..., LAT:].reshape(slots * rows, ROPE)
    tail = jnp.concatenate([rope, jnp.zeros_like(rope)], axis=1)
    for buffer in range(2):
        keys[buffer, :, NOPE:] = tail
    ahead = lax.broadcasted_iota(jnp.int32, (query_count, rows), 1) - lax.broadcasted_iota(
        jnp.int32, (query_count, rows), 0
    )
    limits = [start_ref[0] - order_ref[me ^ slot] * rows for slot in range(slots)]
    first = pair * depth
    place = 0
    if which == 1:
        group = lax.axis_index("groups")
        out_ref[:, pl.ds(pl.multiple_of(group * pair * VD, pair * VD), pair * VD)] = done_ref[...]
        place = pl.multiple_of((1 - group) * pair * VD, pair * VD)
    results = []
    for member in range(pair):
        head = which * pair + member
        buffer = member % 2
        weight = weight_ref[:, member * depth:(member + 1) * depth, :].reshape(LAT, width)
        for begin in range(0, slots * rows, CHUNK):
            part = pl.ds(begin, CHUNK)
            held = latent[begin // rows:(begin + CHUNK) // rows, :, :, :LAT].reshape(CHUNK, LAT)
            projected = jnp.dot(held, weight, preferred_element_type=jnp.float32)
            projected = projected.astype(jnp.bfloat16)
            keys[buffer, part, :NOPE] = projected[:, :NOPE]
            values[buffer, part, :] = projected[:, NOPE:]
        begin = first + which * query_rows
        part = packed_ref[:, begin:begin + query_rows, member * NOPE:(member + 1) * NOPE]
        part = part.reshape(query_count, NOPE)
        begin = first + 2 * query_rows
        turned = packed_ref[:, begin:begin + query_rows, head * ROPE:(head + 1) * ROPE]
        turned = turned.reshape(query_count, ROPE)
        query = jnp.concatenate([part, turned, jnp.zeros_like(turned)], axis=1)
        scores = lax.dot_general(
            query, keys[buffer], (((1,), (1,)), ((), ())), preferred_element_type=jnp.float32
        )
        scores = jnp.concatenate(
            [
                jnp.where(
                    ahead <= limits[slot], scores[:, slot * rows:(slot + 1) * rows], HIDDEN
                )
                for slot in range(slots)
            ],
            axis=1,
        )
        top = jnp.max(scores, axis=1, keepdims=True)
        probs = jnp.exp2((scores - top) * scale)
        totals = jnp.sum(probs, axis=1, keepdims=True)
        result = jnp.dot(probs.astype(jnp.bfloat16), values[buffer], preferred_element_type=jnp.float32)
        results.append((result / totals).astype(jnp.bfloat16))
    out_ref[:, pl.ds(place, pair * VD)] = jnp.concatenate(results, axis=1)


def split_by_heads(contexts, cores, queries, latent_cache, kv_weight, block_order, span_start):
    query_rows, head_count, query_width = queries.shape
    heads = head_count // contexts
    pair = heads // 2
    rows = latent_cache.shape[0]
    half = rows // cores
    depth = kv_weight.shape[0]
    width = NOPE + VD
    group = lax.axis_index("groups")

    def swap(array, bit):
        return lax.ppermute(array, "ctx", [(i, i ^ bit) for i in range(contexts)])

    weight = kv_weight.reshape(depth, contexts, 2, pair, width)
    weight = lax.dynamic_index_in_dim(weight, group, 2, keepdims=False)
    weight = weight.transpose(1, 2, 0, 3).reshape(contexts, pair * depth, width)
    query = queries.reshape(query_rows, contexts, 2, pair, query_width)
    query = jnp.where(group == 0, query, query[:, :, ::-1])
    straight = query[..., :NOPE].transpose(1, 2, 0, 3, 4)
    straight = straight.reshape(contexts, 2 * query_rows, pair * NOPE)
    turned = query[..., NOPE:].transpose(1, 0, 2, 3, 4)
    turned = turned.reshape(contexts, query_rows, heads * ROPE)
    packed = jnp.concatenate([weight, straight, turned], axis=1)
    def trade(array):
        return lax.ppermute(array, "tp", [(0, 1), (1, 0)])

    core = lax.axis_index("tp")
    held = {0: lax.dynamic_slice_in_dim(latent_cache, core * half, half, 0)}
    for slot, source, bit in EARLY:
        held[slot] = swap(held[source], bit)
    waited = lax.optimization_barrier((packed, latent_cache, held[4], held[1], held[2]))
    packed, latent_cache, held[4], held[1], held[2] = waited
    packed = lax.all_to_all(packed, "ctx", 0, 0, tiled=True)
    for slot, source, bit in LATE:
        held[slot] = swap(held[source], bit)
    near = contexts // 2
    close = jnp.stack([held[slot] for slot in range(1, near)])
    waited = lax.optimization_barrier((packed, held[3], held[5], held[6]))
    packed, held[3], held[5], held[6] = waited
    other = lax.ppermute(packed[:, :pair * depth], "groups", [(0, 1), (1, 0)])
    far = jnp.stack([held[slot] for slot in range(near, contexts)])
    own = latent_cache.reshape(cores, half, latent_cache.shape[1])
    close_other = jnp.stack([trade(held[slot]) for slot in range(1, near)])
    far_other = jnp.stack([trade(held[slot]) for slot in range(near, contexts)])
    pieces = [own, close, close_other, far, far_other]

    total_rows = contexts * rows
    query_count = contexts * query_rows
    anywhere = pl.BlockSpec(memory_space=pl.ANY)
    on_chip = pl.BlockSpec(memory_space=pltpu.VMEM)
    scalars = pl.BlockSpec(memory_space=pltpu.SMEM)

    def attend(which, out_heads, operands):
        return pl.pallas_call(
            functools.partial(attend_kernel, contexts, rows, pair, which),
            out_shape=jax.ShapeDtypeStruct((query_count, out_heads * VD), jnp.bfloat16),
            in_specs=[scalars, scalars] + [on_chip] * len(operands) + [anywhere] * len(pieces),
            out_specs=on_chip,
            scratch_shapes=[
                pltpu.VMEM((contexts, cores, half, LAT + ROPE), jnp.bfloat16),
                pltpu.VMEM((2, total_rows, 256), jnp.bfloat16),
                pltpu.VMEM((2, total_rows, VD), jnp.bfloat16),
                pltpu.SemaphoreType.DMA((len(pieces),)),
            ],
            compiler_params=pltpu.CompilerParams(vmem_limit_bytes=16 * 2**20),
            cost_estimate=pl.CostEstimate(flops=1048576, bytes_accessed=1 << 20, transcendentals=0),
            name="attend_" + ("first", "second")[which],
        )(block_order, span_start, *operands, *pieces)

    attended = attend(0, pair, [packed])
    attended = attend(1, heads, [packed, other, attended])
    attended = attended.reshape(contexts, query_rows, heads * VD)
    attended = lax.all_to_all(attended, "ctx", 0, 0, tiled=True)
    attended = attended.reshape(contexts, query_rows, heads, VD).transpose(1, 0, 2, 3)
    return attended.reshape(query_rows, head_count, VD)


def tile_update(running, tile_rows, tile_positions, gathered_queries, weight_matrix, query_last):
    row_max, row_total, accum = running
    softmax_scale = 1.0 / math.sqrt(NOPE + ROPE)
    head_count = gathered_queries.shape[1]
    latent = tile_rows[:, :LAT]
    rope_part = tile_rows[:, LAT:]
    key_value = jnp.dot(latent, weight_matrix, preferred_element_type=jnp.float32).astype(
        jnp.bfloat16
    )
    key_value = key_value.reshape(tile_rows.shape[0], head_count, NOPE + VD)
    scores = jnp.einsum(
        "qhc,khc->hqk",
        gathered_queries[:, :, :NOPE],
        key_value[:, :, :NOPE],
        preferred_element_type=jnp.float32,
    )
    scores = scores + jnp.einsum(
        "qhr,kr->hqk", gathered_queries[:, :, NOPE:], rope_part, preferred_element_type=jnp.float32
    )
    scores = scores * softmax_scale
    visible = (tile_positions[None, :] <= query_last[:, None])[None]
    scores = jnp.where(visible, scores, jnp.float32(-1e30))
    new_max = jnp.maximum(row_max, jnp.max(scores, axis=2))
    weights = jnp.where(visible, jnp.exp(scores - new_max[:, :, None]), jnp.float32(0.0))
    row_total = jnp.sum(weights, axis=2)
    accum = jnp.einsum(
        "hqk,khv->hqv",
        weights.astype(jnp.bfloat16),
        key_value[:, :, NOPE:],
        preferred_element_type=jnp.float32,
    )
    return (new_max, row_total, accum)


def split_by_context(queries, latent_cache, kv_weight, block_order, span_start):
    shard_index = lax.axis_index("ctx")
    gathered_queries = lax.all_gather(queries, "ctx", axis=0, tiled=True)
    full_weight = lax.all_gather(kv_weight, "ctx", axis=0, tiled=True)
    head_count = full_weight.shape[1]
    weight_matrix = full_weight.reshape(LAT, head_count * (NOPE + VD))
    row_count = latent_cache.shape[0]
    own_block = lax.dynamic_index_in_dim(block_order, shard_index, 0, keepdims=False)
    key_positions = own_block * row_count + jnp.arange(row_count, dtype=jnp.int32)
    query_count = gathered_queries.shape[0]
    query_last = span_start[0] + jnp.arange(query_count, dtype=jnp.int32)
    final_position = span_start[0] + query_count - 1
    running = (
        jnp.full((head_count, query_count), -1e30, jnp.float32),
        jnp.zeros((head_count, query_count), jnp.float32),
        jnp.zeros((head_count, query_count, VD), jnp.float32),
    )
    running = lax.cond(
        key_positions[0] <= final_position,
        lambda current, rows_now=latent_cache, places=key_positions: tile_update(
            current, rows_now, places, gathered_queries, weight_matrix, query_last
        ),
        lambda current: current,
        running,
    )
    row_max, row_total, accum = running
    parts_accum, parts_max, parts_total = (
        lax.all_to_all(
            accum[:, :, None, :].astype(jnp.bfloat16),
            "ctx",
            split_axis=1,
            concat_axis=2,
            tiled=True,
        ).astype(jnp.float32),
        lax.all_to_all(
            row_max[:, :, None].astype(jnp.bfloat16), "ctx", split_axis=1, concat_axis=2, tiled=True
        ).astype(jnp.float32),
        lax.all_to_all(
            row_total[:, :, None].astype(jnp.bfloat16),
            "ctx",
            split_axis=1,
            concat_axis=2,
            tiled=True,
        ).astype(jnp.float32),
    )
    overall = jnp.max(parts_max, axis=2, keepdims=True)
    factor = jnp.exp(parts_max - overall)
    denominator = jnp.sum(factor * parts_total, axis=2)
    numerator = jnp.sum(factor[:, :, :, None] * parts_accum, axis=2)
    result = (numerator / denominator[:, :, None]).astype(jnp.bfloat16)
    return jnp.transpose(result, (1, 0, 2))


def solution(mesh):
    contexts = mesh.shape["ctx"]
    cores = mesh.shape["tp"]

    def local(queries, latent_cache, kv_weight, block_order, span_start):
        arrays = (queries, latent_cache, kv_weight, block_order, span_start)
        paired = queries.shape[1] % (2 * contexts) == 0 and contexts == 8
        if paired and cores == 2 and mesh.shape["groups"] == 2:
            return split_by_heads(contexts, cores, *arrays)
        return split_by_context(*arrays)

    return jax.shard_map(
        local,
        mesh=mesh,
        in_specs=(
            P(("groups", "ctx"), "tp", None),
            P(("groups", "ctx"), None),
            P("ctx", "tp", None),
            P("groups"),
            P("groups"),
        ),
        out_specs=P(("groups", "ctx"), "tp", None),
        check_vma=False,
    )
```

```python
import functools
import math

import jax
import jax.numpy as jnp
from jax import lax
from jax.experimental import pallas as pl
from jax.experimental.pallas import tpu as pltpu
from jax.sharding import PartitionSpec as P

LAT = 512
ROPE = 64
NOPE = 128
VD = 128
HIDDEN = -1e30
CHUNK = 512
EARLY = ((4, 0, 4), (1, 0, 1), (2, 0, 2))
LATE = ((3, 2, 1), (5, 4, 1), (6, 4, 2), (7, 5, 2))


def attend_kernel(slots, rows, pair, which, *refs):
    order_ref, start_ref, packed_ref = refs[:3]
    if which == 0:
        weight_ref = packed_ref
        refs = refs[3:]
    else:
        weight_ref, done_ref = refs[3:5]
        refs = refs[5:]
    piece_refs = refs[:5]
    out_ref, latent, keys, values, sems = refs[5:]
    near = slots // 2
    me = lax.axis_index("ctx")
    core = lax.axis_index("tp")
    places = [
        latent.at[0],
        latent.at[pl.ds(1, near - 1), core],
        latent.at[pl.ds(1, near - 1), 1 - core],
        latent.at[pl.ds(near, near), core],
        latent.at[pl.ds(near, near), 1 - core],
    ]
    copies = [
        pltpu.make_async_copy(piece, place, sems.at[index])
        for index, (piece, place) in enumerate(zip(piece_refs, places))
    ]
    for copy in copies:
        copy.start()
    for copy in copies:
        copy.wait()
    width = NOPE + VD
    depth = LAT // slots
    query_rows = (packed_ref.shape[1] - pair * depth) // 3
    query_count = slots * query_rows
    scale = math.log2(math.e) / math.sqrt(NOPE + ROPE)
    rope = latent[..., LAT:].reshape(slots * rows, ROPE)
    tail = jnp.concatenate([rope, jnp.zeros_like(rope)], axis=1)
    for buffer in range(2):
        keys[buffer, :, NOPE:] = tail
    ahead = lax.broadcasted_iota(jnp.int32, (query_count, rows), 1) - lax.broadcasted_iota(
        jnp.int32, (query_count, rows), 0
    )
    limits = [start_ref[0] - order_ref[me ^ slot] * rows for slot in range(slots)]
    first = pair * depth
    place = 0
    if which == 1:
        group = lax.axis_index("groups")
        out_ref[:, pl.ds(pl.multiple_of(group * pair * VD, pair * VD), pair * VD)] = done_ref[...]
        place = pl.multiple_of((1 - group) * pair * VD, pair * VD)
    results = []
    for member in range(pair):
        head = which * pair + member
        buffer = member % 2
        weight = weight_ref[:, member * depth:(member + 1) * depth, :].reshape(LAT, width)
        for begin in range(0, slots * rows, CHUNK):
            part = pl.ds(begin, CHUNK)
            held = latent[begin // rows:(begin + CHUNK) // rows, :, :, :LAT].reshape(CHUNK, LAT)
            projected = jnp.dot(held, weight, preferred_element_type=jnp.float32)
            projected = projected.astype(jnp.bfloat16)
            keys[buffer, part, :NOPE] = projected[:, :NOPE]
            values[buffer, part, :] = projected[:, NOPE:]
        begin = first + which * query_rows
        part = packed_ref[:, begin:begin + query_rows, member * NOPE:(member + 1) * NOPE]
        part = part.reshape(query_count, NOPE)
        begin = first + 2 * query_rows
        turned = packed_ref[:, begin:begin + query_rows, head * ROPE:(head + 1) * ROPE]
        turned = turned.reshape(query_count, ROPE)
        query = jnp.concatenate([part, turned, jnp.zeros_like(turned)], axis=1)
        scores = lax.dot_general(
            query, keys[buffer], (((1,), (1,)), ((), ())), preferred_element_type=jnp.float32
        )
        scores = jnp.concatenate(
            [
                jnp.where(
                    ahead <= limits[slot], scores[:, slot * rows:(slot + 1) * rows], HIDDEN
                )
                for slot in range(slots)
            ],
            axis=1,
        )
        top = jnp.max(scores, axis=1, keepdims=True)
        probs = jnp.exp2((scores - top) * scale)
        totals = jnp.sum(probs, axis=1, keepdims=True)
        result = jnp.dot(probs.astype(jnp.bfloat16), values[buffer], preferred_element_type=jnp.float32)
        results.append((result / totals).astype(jnp.bfloat16))
    out_ref[:, pl.ds(place, pair * VD)] = jnp.concatenate(results, axis=1)


def split_by_heads(contexts, cores, queries, latent_cache, kv_weight, block_order, span_start):
    query_rows, head_count, query_width = queries.shape
    heads = head_count // contexts
    pair = heads // 2
    rows = latent_cache.shape[0]
    half = rows // cores
    depth = kv_weight.shape[0]
    width = NOPE + VD
    group = lax.axis_index("groups")

    def swap(array, bit):
        return lax.ppermute(array, "ctx", [(i, i ^ bit) for i in range(contexts)])

    weight = kv_weight.reshape(depth, contexts, 2, pair, width)
    weight = lax.dynamic_index_in_dim(weight, group, 2, keepdims=False)
    weight = weight.transpose(1, 2, 0, 3).reshape(contexts, pair * depth, width)
    query = queries.reshape(query_rows, contexts, 2, pair, query_width)
    query = jnp.where(group == 0, query, query[:, :, ::-1])
    straight = query[..., :NOPE].transpose(1, 2, 0, 3, 4)
    straight = straight.reshape(contexts, 2 * query_rows, pair * NOPE)
    turned = query[..., NOPE:].transpose(1, 0, 2, 3, 4)
    turned = turned.reshape(contexts, query_rows, heads * ROPE)
    packed = jnp.concatenate([weight, straight, turned], axis=1)

    def trade(array):
        return lax.ppermute(array, "tp", [(0, 1), (1, 0)])

    core = lax.axis_index("tp")
    held = {0: lax.dynamic_slice_in_dim(latent_cache, core * half, half, 0)}
    for slot, source, bit in EARLY:
        held[slot] = swap(held[source], bit)
    waited = lax.optimization_barrier((packed, latent_cache, held[4], held[1], held[2]))
    packed, latent_cache, held[4], held[1], held[2] = waited
    packed = lax.all_to_all(packed, "ctx", 0, 0, tiled=True)
    for slot, source, bit in LATE:
        held[slot] = swap(held[source], bit)
    near = contexts // 2
    close = jnp.stack([held[slot] for slot in range(1, near)])
    other = lax.ppermute(packed[:, :pair * depth], "groups", [(0, 1), (1, 0)])
    far = jnp.stack([held[slot] for slot in range(near, contexts)])
    own = latent_cache.reshape(cores, half, latent_cache.shape[1])
    close_other = jnp.stack([trade(held[slot]) for slot in range(1, near)])
    far_other = jnp.stack([trade(held[slot]) for slot in range(near, contexts)])
    pieces = [own, close, close_other, far, far_other]

    total_rows = contexts * rows
    query_count = contexts * query_rows
    anywhere = pl.BlockSpec(memory_space=pl.ANY)
    on_chip = pl.BlockSpec(memory_space=pltpu.VMEM)
    scalars = pl.BlockSpec(memory_space=pltpu.SMEM)

    def attend(which, out_heads, operands):
        return pl.pallas_call(
            functools.partial(attend_kernel, contexts, rows, pair, which),
            out_shape=jax.ShapeDtypeStruct((query_count, out_heads * VD), jnp.bfloat16),
            in_specs=[scalars, scalars] + [on_chip] * len(operands) + [anywhere] * len(pieces),
            out_specs=on_chip,
            scratch_shapes=[
                pltpu.VMEM((contexts, cores, half, LAT + ROPE), jnp.bfloat16),
                pltpu.VMEM((2, total_rows, 256), jnp.bfloat16),
                pltpu.VMEM((2, total_rows, VD), jnp.bfloat16),
                pltpu.SemaphoreType.DMA((len(pieces),)),
            ],
            compiler_params=pltpu.CompilerParams(vmem_limit_bytes=16 * 2**20),
            cost_estimate=pl.CostEstimate(flops=1048576, bytes_accessed=1 << 20, transcendentals=0),
            name="attend_" + ("first", "second")[which],
        )(block_order, span_start, *operands, *pieces)

    attended = attend(0, pair, [packed])
    attended = attend(1, heads, [packed, other, attended])
    attended = attended.reshape(contexts, query_rows, heads * VD)
    attended = lax.all_to_all(attended, "ctx", 0, 0, tiled=True)
    attended = attended.reshape(contexts, query_rows, heads, VD).transpose(1, 0, 2, 3)
    return attended.reshape(query_rows, head_count, VD)


def tile_update(running, tile_rows, tile_positions, gathered_queries, weight_matrix, query_last):
    row_max, row_total, accum = running
    softmax_scale = 1.0 / math.sqrt(NOPE + ROPE)
    head_count = gathered_queries.shape[1]
    latent = tile_rows[:, :LAT]
    rope_part = tile_rows[:, LAT:]
    key_value = jnp.dot(latent, weight_matrix, preferred_element_type=jnp.float32).astype(
        jnp.bfloat16
    )
    key_value = key_value.reshape(tile_rows.shape[0], head_count, NOPE + VD)
    scores = jnp.einsum(
        "qhc,khc->hqk",
        gathered_queries[:, :, :NOPE],
        key_value[:, :, :NOPE],
        preferred_element_type=jnp.float32,
    )
    scores = scores + jnp.einsum(
        "qhr,kr->hqk", gathered_queries[:, :, NOPE:], rope_part, preferred_element_type=jnp.float32
    )
    scores = scores * softmax_scale
    visible = (tile_positions[None, :] <= query_last[:, None])[None]
    scores = jnp.where(visible, scores, jnp.float32(-1e30))
    new_max = jnp.maximum(row_max, jnp.max(scores, axis=2))
    weights = jnp.where(visible, jnp.exp(scores - new_max[:, :, None]), jnp.float32(0.0))
    row_total = jnp.sum(weights, axis=2)
    accum = jnp.einsum(
        "hqk,khv->hqv",
        weights.astype(jnp.bfloat16),
        key_value[:, :, NOPE:],
        preferred_element_type=jnp.float32,
    )
    return (new_max, row_total, accum)


def split_by_context(queries, latent_cache, kv_weight, block_order, span_start):
    shard_index = lax.axis_index("ctx")
    gathered_queries = lax.all_gather(queries, "ctx", axis=0, tiled=True)
    full_weight = lax.all_gather(kv_weight, "ctx", axis=0, tiled=True)
    head_count = full_weight.shape[1]
    weight_matrix = full_weight.reshape(LAT, head_count * (NOPE + VD))
    row_count = latent_cache.shape[0]
    own_block = lax.dynamic_index_in_dim(block_order, shard_index, 0, keepdims=False)
    key_positions = own_block * row_count + jnp.arange(row_count, dtype=jnp.int32)
    query_count = gathered_queries.shape[0]
    query_last = span_start[0] + jnp.arange(query_count, dtype=jnp.int32)
    final_position = span_start[0] + query_count - 1
    running = (
        jnp.full((head_count, query_count), -1e30, jnp.float32),
        jnp.zeros((head_count, query_count), jnp.float32),
        jnp.zeros((head_count, query_count, VD), jnp.float32),
    )
    running = lax.cond(
        key_positions[0] <= final_position,
        lambda current, rows_now=latent_cache, places=key_positions: tile_update(
            current, rows_now, places, gathered_queries, weight_matrix, query_last
        ),
        lambda current: current,
        running,
    )
    row_max, row_total, accum = running
    parts_accum, parts_max, parts_total = (
        lax.all_to_all(
            accum[:, :, None, :].astype(jnp.bfloat16),
            "ctx",
            split_axis=1,
            concat_axis=2,
            tiled=True,
        ).astype(jnp.float32),
        lax.all_to_all(
            row_max[:, :, None].astype(jnp.bfloat16), "ctx", split_axis=1, concat_axis=2, tiled=True
        ).astype(jnp.float32),
        lax.all_to_all(
            row_total[:, :, None].astype(jnp.bfloat16),
            "ctx",
            split_axis=1,
            concat_axis=2,
            tiled=True,
        ).astype(jnp.float32),
    )
    overall = jnp.max(parts_max, axis=2, keepdims=True)
    factor = jnp.exp(parts_max - overall)
    denominator = jnp.sum(factor * parts_total, axis=2)
    numerator = jnp.sum(factor[:, :, :, None] * parts_accum, axis=2)
    result = (numerator / denominator[:, :, None]).astype(jnp.bfloat16)
    return jnp.transpose(result, (1, 0, 2))


def solution(mesh):
    contexts = mesh.shape["ctx"]
    cores = mesh.shape["tp"]

    def local(queries, latent_cache, kv_weight, block_order, span_start):
        arrays = (queries, latent_cache, kv_weight, block_order, span_start)
        paired = queries.shape[1] % (2 * contexts) == 0 and contexts == 8
        if paired and cores == 2 and mesh.shape["groups"] == 2:
            return split_by_heads(contexts, cores, *arrays)
        return split_by_context(*arrays)

    return jax.shard_map(
        local,
        mesh=mesh,
        in_specs=(
            P(("groups", "ctx"), "tp", None),
            P(("groups", "ctx"), None),
            P("ctx", "tp", None),
            P("groups"),
            P("groups"),
        ),
        out_specs=P(("groups", "ctx"), "tp", None),
        check_vma=False,
    )
```

```python
import functools
import math

import jax
import jax.numpy as jnp
from jax import lax
from jax.experimental import pallas as pl
from jax.experimental.pallas import tpu as pltpu
from jax.sharding import PartitionSpec as P

LAT = 512
ROPE = 64
NOPE = 128
VD = 128
HIDDEN = -1e30
EARLY = ((4, 0, 4), (1, 0, 1), (2, 0, 2))
LATE = ((3, 2, 1), (5, 4, 1), (6, 4, 2), (7, 5, 2))


def attend_kernel(slots, pair, which, *refs):
    order_ref, start_ref, packed_ref = refs[:3]
    if which == 0:
        weight_ref = packed_ref
        refs = refs[3:]
    else:
        weight_ref, done_ref = refs[3:5]
        refs = refs[5:]
    own_ref, *piece_refs, out_ref = refs
    me = lax.axis_index("ctx")
    core = lax.axis_index("tp")
    rows = own_ref.shape[1]
    half = rows // 2
    width = NOPE + VD
    depth = LAT // slots
    query_rows = (packed_ref.shape[1] - pair * depth) // 3
    query_count = slots * query_rows
    scale = math.log2(math.e) / math.sqrt(NOPE + ROPE)
    first = pair * depth
    weights, queries = [], []
    for member in range(pair):
        head = which * pair + member
        weights.append(weight_ref[:, member * depth:(member + 1) * depth, :].reshape(LAT, width))
        begin = first + which * query_rows
        part = packed_ref[:, begin:begin + query_rows, member * NOPE:(member + 1) * NOPE]
        part = part.reshape(query_count, NOPE)
        begin = first + 2 * query_rows
        turned = packed_ref[:, begin:begin + query_rows, head * ROPE:(head + 1) * ROPE]
        turned = turned.reshape(query_count, ROPE)
        queries.append(jnp.concatenate([part, turned, jnp.zeros_like(turned)], axis=1))
    weights = jnp.concatenate(weights, axis=1).T
    ahead = lax.broadcasted_iota(jnp.int32, (query_count, half), 1) - lax.broadcasted_iota(
        jnp.int32, (query_count, half), 0
    )
    scores = [[] for _ in range(pair)]
    values = [[] for _ in range(pair)]
    for base in range(0, slots, 4):
        parts, visible = [], []
        for slot in range(base, base + 4):
            places = (0, half)
            if slot > 0:
                places = (core * half, (1 - core) * half)
                parts += [piece_refs[2 * slot - 2][...], piece_refs[2 * slot - 1][...]]
            else:
                parts.append(own_ref[...])
            limit = start_ref[0] - order_ref[me ^ slot] * rows
            visible += [ahead <= limit - place for place in places]
        latent = jnp.concatenate(parts, axis=1)
        visible = jnp.concatenate(visible, axis=1)
        projected = jnp.dot(weights, latent[:LAT], preferred_element_type=jnp.float32)
        projected = projected.astype(jnp.bfloat16)
        rope = latent[LAT:]
        for member in range(pair):
            begin = member * width
            keys = jnp.concatenate(
                [projected[begin:begin + NOPE], rope, jnp.zeros_like(rope)], axis=0
            )
            score = jnp.dot(queries[member], keys, preferred_element_type=jnp.float32)
            scores[member].append(jnp.where(visible, score, HIDDEN))
            values[member].append(projected[begin + NOPE:begin + width])
    results = []
    for member in range(pair):
        score = jnp.concatenate(scores[member], axis=1)
        top = jnp.max(score, axis=1, keepdims=True)
        probs = jnp.exp2((score - top) * scale)
        totals = jnp.sum(probs, axis=1, keepdims=True)
        result = lax.dot_general(
            probs.astype(jnp.bfloat16), jnp.concatenate(values[member], axis=1),
            (((1,), (1,)), ((), ())), preferred_element_type=jnp.float32,
        )
        results.append((result / totals).astype(jnp.bfloat16))
    place = 0
    if which == 1:
        group = lax.axis_index("groups")
        out_ref[:, pl.ds(pl.multiple_of(group * pair * VD, pair * VD), pair * VD)] = done_ref[...]
        place = pl.multiple_of((1 - group) * pair * VD, pair * VD)
    out_ref[:, pl.ds(place, pair * VD)] = jnp.concatenate(results, axis=1)


def split_by_heads(contexts, cores, queries, latent_cache, kv_weight, block_order, span_start):
    query_rows, head_count, query_width = queries.shape
    heads = head_count // contexts
    pair = heads // 2
    rows = latent_cache.shape[0]
    half = rows // cores
    depth = kv_weight.shape[0]
    width = NOPE + VD
    group = lax.axis_index("groups")

    def swap(array, bit):
        return lax.ppermute(array, "ctx", [(i, i ^ bit) for i in range(contexts)])

    weight = kv_weight.reshape(depth, contexts, 2, pair, width)
    weight = lax.dynamic_index_in_dim(weight, group, 2, keepdims=False)
    weight = weight.transpose(1, 2, 0, 3).reshape(contexts, pair * depth, width)
    query = queries.reshape(query_rows, contexts, 2, pair, query_width)
    query = jnp.where(group == 0, query, query[:, :, ::-1])
    straight = query[..., :NOPE].transpose(1, 2, 0, 3, 4)
    straight = straight.reshape(contexts, 2 * query_rows, pair * NOPE)
    turned = query[..., NOPE:].transpose(1, 0, 2, 3, 4)
    turned = turned.reshape(contexts, query_rows, heads * ROPE)
    packed = jnp.concatenate([weight, straight, turned], axis=1)

    def trade(array):
        return lax.ppermute(array, "tp", [(0, 1), (1, 0)])

    core = lax.axis_index("tp")
    turned_cache = latent_cache.T
    held = {0: lax.dynamic_slice_in_dim(turned_cache, core * half, half, 1)}
    for slot, source, bit in EARLY:
        held[slot] = swap(held[source], bit)
    waited = lax.optimization_barrier((packed, held[4], held[1], held[2]))
    packed, held[4], held[1], held[2] = waited
    packed = lax.all_to_all(packed, "ctx", 0, 0, tiled=True)
    for slot, source, bit in LATE:
        held[slot] = swap(held[source], bit)
    traded = {slot: trade(held[slot]) for slot in (1, 2)}
    packed, held[3], held[5], held[6], traded[1], traded[2] = lax.optimization_barrier((packed, held[3], held[5], held[6], traded[1], traded[2]))
    other = lax.ppermute(packed[:, :pair * depth], "groups", [(0, 1), (1, 0)])
    pieces = [turned_cache]
    for slot in range(1, contexts):
        pieces += [held[slot], traded.get(slot, None) if slot in traded else trade(held[slot])]

    query_count = contexts * query_rows
    on_chip = pl.BlockSpec(memory_space=pltpu.VMEM)
    scalars = pl.BlockSpec(memory_space=pltpu.SMEM)

    def attend(which, out_heads, operands):
        return pl.pallas_call(
            functools.partial(attend_kernel, contexts, pair, which),
            out_shape=jax.ShapeDtypeStruct((query_count, out_heads * VD), jnp.bfloat16),
            in_specs=[scalars, scalars] + [on_chip] * (len(operands) + len(pieces)),
            out_specs=on_chip,
            compiler_params=pltpu.CompilerParams(vmem_limit_bytes=16 * 2**20),
            cost_estimate=pl.CostEstimate(flops=1048576, bytes_accessed=1 << 20, transcendentals=0),
            name="attend_" + ("first", "second")[which],
        )(block_order, span_start, *operands, *pieces)

    attended = attend(0, pair, [packed])
    attended = attend(1, heads, [packed, other, attended])
    attended = attended.reshape(contexts, query_rows, heads * VD)
    attended = lax.all_to_all(attended, "ctx", 0, 0, tiled=True)
    attended = attended.reshape(contexts, query_rows, heads, VD).transpose(1, 0, 2, 3)
    return attended.reshape(query_rows, head_count, VD)


def tile_update(running, tile_rows, tile_positions, gathered_queries, weight_matrix, query_last):
    row_max, row_total, accum = running
    softmax_scale = 1.0 / math.sqrt(NOPE + ROPE)
    head_count = gathered_queries.shape[1]
    latent = tile_rows[:, :LAT]
    rope_part = tile_rows[:, LAT:]
    key_value = jnp.dot(latent, weight_matrix, preferred_element_type=jnp.float32).astype(
        jnp.bfloat16
    )
    key_value = key_value.reshape(tile_rows.shape[0], head_count, NOPE + VD)
    scores = jnp.einsum(
        "qhc,khc->hqk",
        gathered_queries[:, :, :NOPE],
        key_value[:, :, :NOPE],
        preferred_element_type=jnp.float32,
    )
    scores = scores + jnp.einsum(
        "qhr,kr->hqk", gathered_queries[:, :, NOPE:], rope_part, preferred_element_type=jnp.float32
    )
    scores = scores * softmax_scale
    visible = (tile_positions[None, :] <= query_last[:, None])[None]
    scores = jnp.where(visible, scores, jnp.float32(-1e30))
    new_max = jnp.maximum(row_max, jnp.max(scores, axis=2))
    weights = jnp.where(visible, jnp.exp(scores - new_max[:, :, None]), jnp.float32(0.0))
    row_total = jnp.sum(weights, axis=2)
    accum = jnp.einsum(
        "hqk,khv->hqv",
        weights.astype(jnp.bfloat16),
        key_value[:, :, NOPE:],
        preferred_element_type=jnp.float32,
    )
    return (new_max, row_total, accum)


def split_by_context(queries, latent_cache, kv_weight, block_order, span_start):
    shard_index = lax.axis_index("ctx")
    gathered_queries = lax.all_gather(queries, "ctx", axis=0, tiled=True)
    full_weight = lax.all_gather(kv_weight, "ctx", axis=0, tiled=True)
    head_count = full_weight.shape[1]
    weight_matrix = full_weight.reshape(LAT, head_count * (NOPE + VD))
    row_count = latent_cache.shape[0]
    own_block = lax.dynamic_index_in_dim(block_order, shard_index, 0, keepdims=False)
    key_positions = own_block * row_count + jnp.arange(row_count, dtype=jnp.int32)
    query_count = gathered_queries.shape[0]
    query_last = span_start[0] + jnp.arange(query_count, dtype=jnp.int32)
    final_position = span_start[0] + query_count - 1
    running = (
        jnp.full((head_count, query_count), -1e30, jnp.float32),
        jnp.zeros((head_count, query_count), jnp.float32),
        jnp.zeros((head_count, query_count, VD), jnp.float32),
    )
    running = lax.cond(
        key_positions[0] <= final_position,
        lambda current, rows_now=latent_cache, places=key_positions: tile_update(
            current, rows_now, places, gathered_queries, weight_matrix, query_last
        ),
        lambda current: current,
        running,
    )
    row_max, row_total, accum = running
    parts_accum, parts_max, parts_total = (
        lax.all_to_all(
            accum[:, :, None, :].astype(jnp.bfloat16),
            "ctx",
            split_axis=1,
            concat_axis=2,
            tiled=True,
        ).astype(jnp.float32),
        lax.all_to_all(
            row_max[:, :, None].astype(jnp.bfloat16), "ctx", split_axis=1, concat_axis=2, tiled=True
        ).astype(jnp.float32),
        lax.all_to_all(
            row_total[:, :, None].astype(jnp.bfloat16),
            "ctx",
            split_axis=1,
            concat_axis=2,
            tiled=True,
        ).astype(jnp.float32),
    )
    overall = jnp.max(parts_max, axis=2, keepdims=True)
    factor = jnp.exp(parts_max - overall)
    denominator = jnp.sum(factor * parts_total, axis=2)
    numerator = jnp.sum(factor[:, :, :, None] * parts_accum, axis=2)
    result = (numerator / denominator[:, :, None]).astype(jnp.bfloat16)
    return jnp.transpose(result, (1, 0, 2))


def solution(mesh):
    contexts = mesh.shape["ctx"]
    cores = mesh.shape["tp"]

    def local(queries, latent_cache, kv_weight, block_order, span_start):
        arrays = (queries, latent_cache, kv_weight, block_order, span_start)
        paired = queries.shape[1] % (2 * contexts) == 0 and contexts == 8
        if paired and cores == 2 and mesh.shape["groups"] == 2:
            return split_by_heads(contexts, cores, *arrays)
        return split_by_context(*arrays)

    return jax.shard_map(
        local,
        mesh=mesh,
        in_specs=(
            P(("groups", "ctx"), "tp", None),
            P(("groups", "ctx"), None),
            P("ctx", "tp", None),
            P("groups"),
            P("groups"),
        ),
        out_specs=P(("groups", "ctx"), "tp", None),
        check_vma=False,
    )
```

```python
import functools
import math

import jax
import jax.numpy as jnp
from jax import lax
from jax.experimental import pallas as pl
from jax.experimental.pallas import tpu as pltpu
from jax.sharding import PartitionSpec as P

LAT = 512
ROPE = 64
NOPE = 128
VD = 128
HIDDEN = -1e30
EARLY = ((4, 0, 4), (1, 0, 1), (2, 0, 2))
LATE = ((3, 2, 1), (5, 4, 1), (6, 4, 2), (7, 5, 2))


def attend_kernel(slots, pair, which, *refs):
    me = lax.axis_index("ctx")
    order_ref, start_ref, packed_ref = refs[:3]
    if which == 0:
        weight_ref = packed_ref
        refs = refs[3:]
    else:
        kept_ref, others_ref, done_ref = refs[3:6]
        *refs, weight_ref = refs[6:]
        weight_ref[me] = kept_ref[...]
        for step in range(1, slots):
            weight_ref[lax.rem(me + step, slots)] = others_ref[step - 1]
    own_ref, *piece_refs, out_ref = refs
    core = lax.axis_index("tp")
    rows = own_ref.shape[1]
    half = rows // 2
    width = NOPE + VD
    depth = LAT // slots
    query_rows = (packed_ref.shape[1] - pair * depth) // 3
    query_count = slots * query_rows
    scale = math.log2(math.e) / math.sqrt(NOPE + ROPE)
    first = pair * depth
    weights, queries = [], []
    for member in range(pair):
        head = which * pair + member
        weights.append(weight_ref[:, member * depth:(member + 1) * depth, :].reshape(LAT, width))
        begin = first + which * query_rows
        part = packed_ref[:, begin:begin + query_rows, member * NOPE:(member + 1) * NOPE]
        part = part.reshape(query_count, NOPE)
        begin = first + 2 * query_rows
        turned = packed_ref[:, begin:begin + query_rows, head * ROPE:(head + 1) * ROPE]
        turned = turned.reshape(query_count, ROPE)
        queries.append(jnp.concatenate([part, turned, jnp.zeros_like(turned)], axis=1))
    weights = jnp.concatenate(weights, axis=1).T
    ahead = lax.broadcasted_iota(jnp.int32, (query_count, half), 1) - lax.broadcasted_iota(
        jnp.int32, (query_count, half), 0
    )
    scores = [[] for _ in range(pair)]
    values = [[] for _ in range(pair)]
    for base in range(0, slots, 4):
        parts, visible = [], []
        for slot in range(base, base + 4):
            places = (0, half)
            if slot > 0:
                places = (core * half, (1 - core) * half)
                parts += [piece_refs[2 * slot - 2][...], piece_refs[2 * slot - 1][...]]
            else:
                parts.append(own_ref[...])
            limit = start_ref[0] - order_ref[me ^ slot] * rows
            visible += [ahead <= limit - place for place in places]
        latent = jnp.concatenate(parts, axis=1)
        visible = jnp.concatenate(visible, axis=1)
        projected = jnp.dot(weights, latent[:LAT], preferred_element_type=jnp.float32)
        projected = projected.astype(jnp.bfloat16)
        rope = latent[LAT:]
        for member in range(pair):
            begin = member * width
            keys = jnp.concatenate(
                [projected[begin:begin + NOPE], rope, jnp.zeros_like(rope)], axis=0
            )
            score = jnp.dot(queries[member], keys, preferred_element_type=jnp.float32)
            scores[member].append(jnp.where(visible, score, HIDDEN))
            values[member].append(projected[begin + NOPE:begin + width])
    results = []
    for member in range(pair):
        score = jnp.concatenate(scores[member], axis=1)
        top = jnp.max(score, axis=1, keepdims=True)
        probs = jnp.exp2((score - top) * scale)
        totals = jnp.sum(probs, axis=1, keepdims=True)
        result = lax.dot_general(
            probs.astype(jnp.bfloat16), jnp.concatenate(values[member], axis=1),
            (((1,), (1,)), ((), ())), preferred_element_type=jnp.float32,
        )
        results.append((result / totals).astype(jnp.bfloat16))
    place = 0
    if which == 1:
        group = lax.axis_index("groups")
        out_ref[:, pl.ds(pl.multiple_of(group * pair * VD, pair * VD), pair * VD)] = done_ref[...]
        place = pl.multiple_of((1 - group) * pair * VD, pair * VD)
    out_ref[:, pl.ds(place, pair * VD)] = jnp.concatenate(results, axis=1)


def split_by_heads(contexts, cores, queries, latent_cache, kv_weight, block_order, span_start):
    query_rows, head_count, query_width = queries.shape
    heads = head_count // contexts
    pair = heads // 2
    rows = latent_cache.shape[0]
    half = rows // cores
    depth = kv_weight.shape[0]
    width = NOPE + VD
    group = lax.axis_index("groups")

    def swap(array, bit):
        return lax.ppermute(array, "ctx", [(i, i ^ bit) for i in range(contexts)])

    weight = kv_weight.reshape(depth, contexts, 2, pair, width)
    weight = lax.dynamic_index_in_dim(weight, group, 2, keepdims=False)
    weight = weight.transpose(1, 2, 0, 3).reshape(contexts, pair * depth, width)
    me = lax.axis_index("ctx")
    kept = kv_weight.reshape(depth, contexts, 2, pair, width)
    kept = lax.dynamic_slice(kept, (0, me, 1 - group, 0, 0), (depth, 1, 1, pair, width))
    kept = kept.reshape(depth, pair, width).transpose(1, 0, 2).reshape(pair * depth, width)
    query = queries.reshape(query_rows, contexts, 2, pair, query_width)
    query = jnp.where(group == 0, query, query[:, :, ::-1])
    straight = query[..., :NOPE].transpose(1, 2, 0, 3, 4)
    straight = straight.reshape(contexts, 2 * query_rows, pair * NOPE)
    turned = query[..., NOPE:].transpose(1, 0, 2, 3, 4)
    turned = turned.reshape(contexts, query_rows, heads * ROPE)
    packed = jnp.concatenate([weight, straight, turned], axis=1)

    def trade(array):
        return lax.ppermute(array, "tp", [(0, 1), (1, 0)])

    core = lax.axis_index("tp")
    turned_cache = latent_cache.T
    held = {0: lax.dynamic_slice_in_dim(turned_cache, core * half, half, 1)}
    for slot, source, bit in EARLY:
        held[slot] = swap(held[source], bit)
    waited = lax.optimization_barrier((packed, held[4], held[1], held[2]))
    packed, held[4], held[1], held[2] = waited
    packed = lax.all_to_all(packed, "ctx", 0, 0, tiled=True)
    for slot, source, bit in LATE:
        held[slot] = swap(held[source], bit)
    traded = {slot: trade(held[slot]) for slot in (1, 2)}
    packed, kept, held[3], held[5], held[6], traded[1], traded[2] = lax.optimization_barrier((packed, kept, held[3], held[5], held[6], traded[1], traded[2]))
    others = packed[:, :pair * depth]
    others = lax.dynamic_slice_in_dim(
        jnp.concatenate([others, others]), me + 1, contexts - 1, 0
    )
    others = lax.ppermute(others, "groups", [(0, 1), (1, 0)])
    pieces = [turned_cache]
    for slot in range(1, contexts):
        pieces += [held[slot], traded.get(slot, None) if slot in traded else trade(held[slot])]

    query_count = contexts * query_rows
    on_chip = pl.BlockSpec(memory_space=pltpu.VMEM)
    scalars = pl.BlockSpec(memory_space=pltpu.SMEM)

    def attend(which, out_heads, operands):
        return pl.pallas_call(
            functools.partial(attend_kernel, contexts, pair, which),
            out_shape=jax.ShapeDtypeStruct((query_count, out_heads * VD), jnp.bfloat16),
            in_specs=[scalars, scalars] + [on_chip] * (len(operands) + len(pieces)),
            out_specs=on_chip,
            scratch_shapes=[pltpu.VMEM((contexts, pair * depth, width), jnp.bfloat16)] * which,
            compiler_params=pltpu.CompilerParams(vmem_limit_bytes=16 * 2**20),
            cost_estimate=pl.CostEstimate(flops=1048576, bytes_accessed=1 << 20, transcendentals=0),
            name="attend_" + ("first", "second")[which],
        )(block_order, span_start, *operands, *pieces)

    attended = attend(0, pair, [packed])
    attended = attend(1, heads, [packed, kept, others, attended])
    attended = attended.reshape(contexts, query_rows, heads * VD)
    attended = lax.all_to_all(attended, "ctx", 0, 0, tiled=True)
    attended = attended.reshape(contexts, query_rows, heads, VD).transpose(1, 0, 2, 3)
    return attended.reshape(query_rows, head_count, VD)


def tile_update(running, tile_rows, tile_positions, gathered_queries, weight_matrix, query_last):
    row_max, row_total, accum = running
    softmax_scale = 1.0 / math.sqrt(NOPE + ROPE)
    head_count = gathered_queries.shape[1]
    latent = tile_rows[:, :LAT]
    rope_part = tile_rows[:, LAT:]
    key_value = jnp.dot(latent, weight_matrix, preferred_element_type=jnp.float32).astype(
        jnp.bfloat16
    )
    key_value = key_value.reshape(tile_rows.shape[0], head_count, NOPE + VD)
    scores = jnp.einsum(
        "qhc,khc->hqk",
        gathered_queries[:, :, :NOPE],
        key_value[:, :, :NOPE],
        preferred_element_type=jnp.float32,
    )
    scores = scores + jnp.einsum(
        "qhr,kr->hqk", gathered_queries[:, :, NOPE:], rope_part, preferred_element_type=jnp.float32
    )
    scores = scores * softmax_scale
    visible = (tile_positions[None, :] <= query_last[:, None])[None]
    scores = jnp.where(visible, scores, jnp.float32(-1e30))
    new_max = jnp.maximum(row_max, jnp.max(scores, axis=2))
    weights = jnp.where(visible, jnp.exp(scores - new_max[:, :, None]), jnp.float32(0.0))
    row_total = jnp.sum(weights, axis=2)
    accum = jnp.einsum(
        "hqk,khv->hqv",
        weights.astype(jnp.bfloat16),
        key_value[:, :, NOPE:],
        preferred_element_type=jnp.float32,
    )
    return (new_max, row_total, accum)


def split_by_context(queries, latent_cache, kv_weight, block_order, span_start):
    shard_index = lax.axis_index("ctx")
    gathered_queries = lax.all_gather(queries, "ctx", axis=0, tiled=True)
    full_weight = lax.all_gather(kv_weight, "ctx", axis=0, tiled=True)
    head_count = full_weight.shape[1]
    weight_matrix = full_weight.reshape(LAT, head_count * (NOPE + VD))
    row_count = latent_cache.shape[0]
    own_block = lax.dynamic_index_in_dim(block_order, shard_index, 0, keepdims=False)
    key_positions = own_block * row_count + jnp.arange(row_count, dtype=jnp.int32)
    query_count = gathered_queries.shape[0]
    query_last = span_start[0] + jnp.arange(query_count, dtype=jnp.int32)
    final_position = span_start[0] + query_count - 1
    running = (
        jnp.full((head_count, query_count), -1e30, jnp.float32),
        jnp.zeros((head_count, query_count), jnp.float32),
        jnp.zeros((head_count, query_count, VD), jnp.float32),
    )
    running = lax.cond(
        key_positions[0] <= final_position,
        lambda current, rows_now=latent_cache, places=key_positions: tile_update(
            current, rows_now, places, gathered_queries, weight_matrix, query_last
        ),
        lambda current: current,
        running,
    )
    row_max, row_total, accum = running
    parts_accum, parts_max, parts_total = (
        lax.all_to_all(
            accum[:, :, None, :].astype(jnp.bfloat16),
            "ctx",
            split_axis=1,
            concat_axis=2,
            tiled=True,
        ).astype(jnp.float32),
        lax.all_to_all(
            row_max[:, :, None].astype(jnp.bfloat16), "ctx", split_axis=1, concat_axis=2, tiled=True
        ).astype(jnp.float32),
        lax.all_to_all(
            row_total[:, :, None].astype(jnp.bfloat16),
            "ctx",
            split_axis=1,
            concat_axis=2,
            tiled=True,
        ).astype(jnp.float32),
    )
    overall = jnp.max(parts_max, axis=2, keepdims=True)
    factor = jnp.exp(parts_max - overall)
    denominator = jnp.sum(factor * parts_total, axis=2)
    numerator = jnp.sum(factor[:, :, :, None] * parts_accum, axis=2)
    result = (numerator / denominator[:, :, None]).astype(jnp.bfloat16)
    return jnp.transpose(result, (1, 0, 2))


def solution(mesh):
    contexts = mesh.shape["ctx"]
    cores = mesh.shape["tp"]

    def local(queries, latent_cache, kv_weight, block_order, span_start):
        arrays = (queries, latent_cache, kv_weight, block_order, span_start)
        paired = queries.shape[1] % (2 * contexts) == 0 and contexts == 8
        if paired and cores == 2 and mesh.shape["groups"] == 2:
            return split_by_heads(contexts, cores, *arrays)
        return split_by_context(*arrays)

    return jax.shard_map(
        local,
        mesh=mesh,
        in_specs=(
            P(("groups", "ctx"), "tp", None),
            P(("groups", "ctx"), None),
            P("ctx", "tp", None),
            P("groups"),
            P("groups"),
        ),
        out_specs=P(("groups", "ctx"), "tp", None),
        check_vma=False,
    )
```

```python
import functools
import math

import jax
import jax.numpy as jnp
from jax import lax
from jax.experimental import pallas as pl
from jax.experimental.pallas import tpu as pltpu
from jax.sharding import PartitionSpec as P

LAT = 512
ROPE = 64
NOPE = 128
VD = 128
HIDDEN = -1e30
EARLY = ((4, 0, 4), (1, 0, 1), (2, 0, 2))
LATE = ((3, 2, 1), (5, 4, 1), (6, 4, 2), (7, 5, 2))


def attend_kernel(slots, pair, which, *refs):
    me = lax.axis_index("ctx")
    order_ref, start_ref, packed_ref = refs[:3]
    if which == 0:
        weight_ref = packed_ref
        refs = refs[3:]
    else:
        near = slots // 2
        near_refs, (others_ref, done_ref) = refs[3:3 + near], refs[3 + near:5 + near]
        *refs, weight_ref = refs[5 + near:]
        for slot, near_ref in enumerate(near_refs):
            weight_ref[me ^ slot] = near_ref[...]
        weight_ref[pl.ds((me // near ^ 1) * near, near)] = others_ref[...]
    own_ref, *piece_refs, out_ref = refs
    core = lax.axis_index("tp")
    rows = own_ref.shape[1]
    half = rows // 2
    width = NOPE + VD
    depth = LAT // slots
    query_rows = (packed_ref.shape[1] - pair * depth) // 3
    query_count = slots * query_rows
    scale = math.log2(math.e) / math.sqrt(NOPE + ROPE)
    first = pair * depth
    weights, queries = [], []
    for member in range(pair):
        head = which * pair + member
        weights.append(weight_ref[:, member * depth:(member + 1) * depth, :].reshape(LAT, width))
        begin = first + which * query_rows
        part = packed_ref[:, begin:begin + query_rows, member * NOPE:(member + 1) * NOPE]
        part = part.reshape(query_count, NOPE)
        begin = first + 2 * query_rows
        turned = packed_ref[:, begin:begin + query_rows, head * ROPE:(head + 1) * ROPE]
        turned = turned.reshape(query_count, ROPE)
        queries.append(jnp.concatenate([part, turned, jnp.zeros_like(turned)], axis=1))
    weights = jnp.concatenate(weights, axis=1).T
    ahead = lax.broadcasted_iota(jnp.int32, (query_count, half), 1) - lax.broadcasted_iota(
        jnp.int32, (query_count, half), 0
    )
    scores = [[] for _ in range(pair)]
    values = [[] for _ in range(pair)]
    for base in range(0, slots, 4):
        parts, visible = [], []
        for slot in range(base, base + 4):
            places = (0, half)
            if slot > 0:
                places = (core * half, (1 - core) * half)
                parts += [piece_refs[2 * slot - 2][...], piece_refs[2 * slot - 1][...]]
            else:
                parts.append(own_ref[...])
            limit = start_ref[0] - order_ref[me ^ slot] * rows
            visible += [ahead <= limit - place for place in places]
        latent = jnp.concatenate(parts, axis=1)
        visible = jnp.concatenate(visible, axis=1)
        projected = jnp.dot(weights, latent[:LAT], preferred_element_type=jnp.float32)
        projected = projected.astype(jnp.bfloat16)
        rope = latent[LAT:]
        for member in range(pair):
            begin = member * width
            keys = jnp.concatenate(
                [projected[begin:begin + NOPE], rope, jnp.zeros_like(rope)], axis=0
            )
            score = jnp.dot(queries[member], keys, preferred_element_type=jnp.float32)
            scores[member].append(jnp.where(visible, score, HIDDEN))
            values[member].append(projected[begin + NOPE:begin + width])
    results = []
    for member in range(pair):
        score = jnp.concatenate(scores[member], axis=1)
        top = jnp.max(score, axis=1, keepdims=True)
        probs = jnp.exp2((score - top) * scale)
        totals = jnp.sum(probs, axis=1, keepdims=True)
        result = lax.dot_general(
            probs.astype(jnp.bfloat16), jnp.concatenate(values[member], axis=1),
            (((1,), (1,)), ((), ())), preferred_element_type=jnp.float32,
        )
        results.append((result / totals).astype(jnp.bfloat16))
    place = 0
    if which == 1:
        group = lax.axis_index("groups")
        out_ref[:, pl.ds(pl.multiple_of(group * pair * VD, pair * VD), pair * VD)] = done_ref[...]
        place = pl.multiple_of((1 - group) * pair * VD, pair * VD)
    out_ref[:, pl.ds(place, pair * VD)] = jnp.concatenate(results, axis=1)


def split_by_heads(contexts, cores, queries, latent_cache, kv_weight, block_order, span_start):
    query_rows, head_count, query_width = queries.shape
    heads = head_count // contexts
    pair = heads // 2
    rows = latent_cache.shape[0]
    half = rows // cores
    depth = kv_weight.shape[0]
    width = NOPE + VD
    group = lax.axis_index("groups")

    def swap(array, bit):
        return lax.ppermute(array, "ctx", [(i, i ^ bit) for i in range(contexts)])

    weight = kv_weight.reshape(depth, contexts, 2, pair, width)
    weight = lax.dynamic_index_in_dim(weight, group, 2, keepdims=False)
    weight = weight.transpose(1, 2, 0, 3).reshape(contexts, pair * depth, width)
    me = lax.axis_index("ctx")
    by_head = kv_weight.reshape(depth, contexts, 2, pair, width)

    def second_pair(owner):
        part = lax.dynamic_slice(
            by_head, (0, owner, 1 - group, 0, 0), (depth, 1, 1, pair, width)
        )
        part = part.reshape(depth, pair, width).transpose(1, 0, 2)
        return part.reshape(pair * depth, width)

    kept = second_pair(me)
    near = contexts // 2
    beside = {slot: swap(second_pair(me ^ slot), slot) for slot in range(1, near)}
    query = queries.reshape(query_rows, contexts, 2, pair, query_width)
    query = jnp.where(group == 0, query, query[:, :, ::-1])
    straight = query[..., :NOPE].transpose(1, 2, 0, 3, 4)
    straight = straight.reshape(contexts, 2 * query_rows, pair * NOPE)
    turned = query[..., NOPE:].transpose(1, 0, 2, 3, 4)
    turned = turned.reshape(contexts, query_rows, heads * ROPE)
    packed = jnp.concatenate([weight, straight, turned], axis=1)

    def trade(array):
        return lax.ppermute(array, "tp", [(0, 1), (1, 0)])

    core = lax.axis_index("tp")
    turned_cache = latent_cache.T
    held = {0: lax.dynamic_slice_in_dim(turned_cache, core * half, half, 1)}
    for slot, source, bit in EARLY:
        held[slot] = swap(held[source], bit)
    waited = lax.optimization_barrier((packed, held[4], held[1], held[2], beside[1], beside[2]))
    packed, held[4], held[1], held[2], beside[1], beside[2] = waited
    packed = lax.all_to_all(packed, "ctx", 0, 0, tiled=True)
    for slot, source, bit in LATE:
        held[slot] = swap(held[source], bit)
    traded = {slot: trade(held[slot]) for slot in (1, 2)}
    packed, kept, held[3], held[5], held[6], traded[1], traded[2] = lax.optimization_barrier((packed, kept, held[3], held[5], held[6], traded[1], traded[2]))
    others = lax.dynamic_slice_in_dim(packed, (me // near ^ 1) * near, near, 0)[:, :pair * depth]
    others = lax.ppermute(others, "groups", [(0, 1), (1, 0)])
    pieces = [turned_cache]
    for slot in range(1, contexts):
        pieces += [held[slot], traded.get(slot, None) if slot in traded else trade(held[slot])]

    query_count = contexts * query_rows
    on_chip = pl.BlockSpec(memory_space=pltpu.VMEM)
    scalars = pl.BlockSpec(memory_space=pltpu.SMEM)

    def attend(which, out_heads, operands):
        return pl.pallas_call(
            functools.partial(attend_kernel, contexts, pair, which),
            out_shape=jax.ShapeDtypeStruct((query_count, out_heads * VD), jnp.bfloat16),
            in_specs=[scalars, scalars] + [on_chip] * (len(operands) + len(pieces)),
            out_specs=on_chip,
            scratch_shapes=[pltpu.VMEM((contexts, pair * depth, width), jnp.bfloat16)] * which,
            compiler_params=pltpu.CompilerParams(vmem_limit_bytes=16 * 2**20),
            cost_estimate=pl.CostEstimate(flops=1048576, bytes_accessed=1 << 20, transcendentals=0),
            name="attend_" + ("first", "second")[which],
        )(block_order, span_start, *operands, *pieces)

    attended = attend(0, pair, [packed])
    attended = attend(1, heads, [packed, kept, *beside.values(), others, attended])
    attended = attended.reshape(contexts, query_rows, heads * VD)
    attended = lax.all_to_all(attended, "ctx", 0, 0, tiled=True)
    attended = attended.reshape(contexts, query_rows, heads, VD).transpose(1, 0, 2, 3)
    return attended.reshape(query_rows, head_count, VD)


def tile_update(running, tile_rows, tile_positions, gathered_queries, weight_matrix, query_last):
    row_max, row_total, accum = running
    softmax_scale = 1.0 / math.sqrt(NOPE + ROPE)
    head_count = gathered_queries.shape[1]
    latent = tile_rows[:, :LAT]
    rope_part = tile_rows[:, LAT:]
    key_value = jnp.dot(latent, weight_matrix, preferred_element_type=jnp.float32).astype(
        jnp.bfloat16
    )
    key_value = key_value.reshape(tile_rows.shape[0], head_count, NOPE + VD)
    scores = jnp.einsum(
        "qhc,khc->hqk",
        gathered_queries[:, :, :NOPE],
        key_value[:, :, :NOPE],
        preferred_element_type=jnp.float32,
    )
    scores = scores + jnp.einsum(
        "qhr,kr->hqk", gathered_queries[:, :, NOPE:], rope_part, preferred_element_type=jnp.float32
    )
    scores = scores * softmax_scale
    visible = (tile_positions[None, :] <= query_last[:, None])[None]
    scores = jnp.where(visible, scores, jnp.float32(-1e30))
    new_max = jnp.maximum(row_max, jnp.max(scores, axis=2))
    weights = jnp.where(visible, jnp.exp(scores - new_max[:, :, None]), jnp.float32(0.0))
    row_total = jnp.sum(weights, axis=2)
    accum = jnp.einsum(
        "hqk,khv->hqv",
        weights.astype(jnp.bfloat16),
        key_value[:, :, NOPE:],
        preferred_element_type=jnp.float32,
    )
    return (new_max, row_total, accum)


def split_by_context(queries, latent_cache, kv_weight, block_order, span_start):
    shard_index = lax.axis_index("ctx")
    gathered_queries = lax.all_gather(queries, "ctx", axis=0, tiled=True)
    full_weight = lax.all_gather(kv_weight, "ctx", axis=0, tiled=True)
    head_count = full_weight.shape[1]
    weight_matrix = full_weight.reshape(LAT, head_count * (NOPE + VD))
    row_count = latent_cache.shape[0]
    own_block = lax.dynamic_index_in_dim(block_order, shard_index, 0, keepdims=False)
    key_positions = own_block * row_count + jnp.arange(row_count, dtype=jnp.int32)
    query_count = gathered_queries.shape[0]
    query_last = span_start[0] + jnp.arange(query_count, dtype=jnp.int32)
    final_position = span_start[0] + query_count - 1
    running = (
        jnp.full((head_count, query_count), -1e30, jnp.float32),
        jnp.zeros((head_count, query_count), jnp.float32),
        jnp.zeros((head_count, query_count, VD), jnp.float32),
    )
    running = lax.cond(
        key_positions[0] <= final_position,
        lambda current, rows_now=latent_cache, places=key_positions: tile_update(
            current, rows_now, places, gathered_queries, weight_matrix, query_last
        ),
        lambda current: current,
        running,
    )
    row_max, row_total, accum = running
    parts_accum, parts_max, parts_total = (
        lax.all_to_all(
            accum[:, :, None, :].astype(jnp.bfloat16),
            "ctx",
            split_axis=1,
            concat_axis=2,
            tiled=True,
        ).astype(jnp.float32),
        lax.all_to_all(
            row_max[:, :, None].astype(jnp.bfloat16), "ctx", split_axis=1, concat_axis=2, tiled=True
        ).astype(jnp.float32),
        lax.all_to_all(
            row_total[:, :, None].astype(jnp.bfloat16),
            "ctx",
            split_axis=1,
            concat_axis=2,
            tiled=True,
        ).astype(jnp.float32),
    )
    overall = jnp.max(parts_max, axis=2, keepdims=True)
    factor = jnp.exp(parts_max - overall)
    denominator = jnp.sum(factor * parts_total, axis=2)
    numerator = jnp.sum(factor[:, :, :, None] * parts_accum, axis=2)
    result = (numerator / denominator[:, :, None]).astype(jnp.bfloat16)
    return jnp.transpose(result, (1, 0, 2))


def solution(mesh):
    contexts = mesh.shape["ctx"]
    cores = mesh.shape["tp"]

    def local(queries, latent_cache, kv_weight, block_order, span_start):
        arrays = (queries, latent_cache, kv_weight, block_order, span_start)
        paired = queries.shape[1] % (2 * contexts) == 0 and contexts == 8
        if paired and cores == 2 and mesh.shape["groups"] == 2:
            return split_by_heads(contexts, cores, *arrays)
        return split_by_context(*arrays)

    return jax.shard_map(
        local,
        mesh=mesh,
        in_specs=(
            P(("groups", "ctx"), "tp", None),
            P(("groups", "ctx"), None),
            P("ctx", "tp", None),
            P("groups"),
            P("groups"),
        ),
        out_specs=P(("groups", "ctx"), "tp", None),
        check_vma=False,
    )
```

```python
import functools
import math

import jax
import jax.numpy as jnp
from jax import lax
from jax.experimental import pallas as pl
from jax.experimental.pallas import tpu as pltpu
from jax.sharding import PartitionSpec as P

LAT = 512
ROPE = 64
NOPE = 128
VD = 128
HIDDEN = -1e30
EARLY = ((4, 0, 4), (1, 0, 1), (2, 0, 2))
LATE = ((3, 2, 1), (5, 4, 1), (6, 4, 2), (7, 5, 2))


def attend_kernel(slots, pair, which, *refs):
    me = lax.axis_index("ctx")
    order_ref, start_ref, packed_ref = refs[:3]
    if which == 0:
        weight_ref = packed_ref
        refs = refs[3:]
    else:
        near = slots // 2
        near_refs, (others_ref, done_ref) = refs[3:3 + near], refs[3 + near:5 + near]
        *refs, weight_ref = refs[5 + near:]
        for slot, near_ref in enumerate(near_refs):
            weight_ref[me ^ slot] = near_ref[...]
        weight_ref[pl.ds((me // near ^ 1) * near, near)] = others_ref[...]
    own_ref, *piece_refs, out_ref = refs
    core = lax.axis_index("tp")
    rows = own_ref.shape[1]
    half = rows // 2
    width = NOPE + VD
    depth = LAT // slots
    query_rows = (packed_ref.shape[1] - pair * depth) // 3
    query_count = slots * query_rows
    scale = math.log2(math.e) / math.sqrt(NOPE + ROPE)
    first = pair * depth
    weights, queries = [], []
    for member in range(pair):
        head = which * pair + member
        weights.append(weight_ref[:, member * depth:(member + 1) * depth, :].reshape(LAT, width))
        begin = first + which * query_rows
        part = packed_ref[:, begin:begin + query_rows, member * NOPE:(member + 1) * NOPE]
        part = part.reshape(query_count, NOPE)
        begin = first + 2 * query_rows
        turned = packed_ref[:, begin:begin + query_rows, head * ROPE:(head + 1) * ROPE]
        turned = turned.reshape(query_count, ROPE)
        queries.append(jnp.concatenate([part, turned, jnp.zeros_like(turned)], axis=1))
    weights = jnp.concatenate(weights, axis=1).T
    ahead = lax.broadcasted_iota(jnp.int32, (query_count, half), 1) - lax.broadcasted_iota(
        jnp.int32, (query_count, half), 0
    )
    scores = [[] for _ in range(pair)]
    values = [[] for _ in range(pair)]
    for base in range(0, slots, 4):
        parts, visible = [], []
        for slot in range(base, base + 4):
            places = (0, half)
            if slot > 0:
                places = (core * half, (1 - core) * half)
                parts += [piece_refs[2 * slot - 2][...], piece_refs[2 * slot - 1][...]]
            else:
                parts.append(own_ref[...])
            limit = start_ref[0] - order_ref[me ^ slot] * rows
            visible += [ahead <= limit - place for place in places]
        latent = jnp.concatenate(parts, axis=1)
        visible = jnp.concatenate(visible, axis=1)
        projected = jnp.dot(weights, latent[:LAT], preferred_element_type=jnp.float32)
        projected = projected.astype(jnp.bfloat16)
        rope = latent[LAT:]
        for member in range(pair):
            begin = member * width
            keys = jnp.concatenate(
                [projected[begin:begin + NOPE], rope, jnp.zeros_like(rope)], axis=0
            )
            score = jnp.dot(queries[member], keys, preferred_element_type=jnp.float32)
            scores[member].append(jnp.where(visible, score, HIDDEN))
            values[member].append(projected[begin + NOPE:begin + width])
    results = []
    for member in range(pair):
        score = jnp.concatenate(scores[member], axis=1)
        top = jnp.max(score, axis=1, keepdims=True)
        probs = jnp.exp2((score - top) * scale)
        totals = jnp.sum(probs, axis=1, keepdims=True)
        result = lax.dot_general(
            probs.astype(jnp.bfloat16), jnp.concatenate(values[member], axis=1),
            (((1,), (1,)), ((), ())), preferred_element_type=jnp.float32,
        )
        results.append((result / totals).astype(jnp.bfloat16))
    place = 0
    if which == 1:
        group = lax.axis_index("groups")
        out_ref[:, pl.ds(pl.multiple_of(group * pair * VD, pair * VD), pair * VD)] = done_ref[...]
        place = pl.multiple_of((1 - group) * pair * VD, pair * VD)
    out_ref[:, pl.ds(place, pair * VD)] = jnp.concatenate(results, axis=1)


def split_by_heads(contexts, cores, queries, latent_cache, kv_weight, block_order, span_start):
    query_rows, head_count, query_width = queries.shape
    heads = head_count // contexts
    pair = heads // 2
    rows = latent_cache.shape[0]
    half = rows // cores
    depth = kv_weight.shape[0]
    width = NOPE + VD
    group = lax.axis_index("groups")

    def swap(array, bit):
        return lax.ppermute(array, "ctx", [(i, i ^ bit) for i in range(contexts)])

    me = lax.axis_index("ctx")
    by_head = kv_weight.reshape(depth, contexts, 2, pair, width)
    weight = lax.dynamic_index_in_dim(by_head, group, 2, keepdims=False)
    weight = weight.transpose(1, 2, 0, 3).reshape(contexts, pair * depth, width)

    def second_pair(owner):
        part = lax.dynamic_slice(
            by_head, (0, owner, 1 - group, 0, 0), (depth, 1, 1, pair, width)
        )
        part = part.reshape(depth, pair, width).transpose(1, 0, 2)
        return part.reshape(pair * depth, width)

    kept = second_pair(me)
    near = contexts // 2
    beside = {slot: swap(second_pair(me ^ slot), slot) for slot in range(1, near)}
    query = queries.reshape(query_rows, contexts, 2, pair, query_width)
    query = jnp.where(group == 0, query, query[:, :, ::-1])
    straight = query[..., :NOPE].transpose(1, 2, 0, 3, 4)
    straight = straight.reshape(contexts, 2 * query_rows, pair * NOPE)
    turned = query[..., NOPE:].transpose(1, 0, 2, 3, 4)
    turned = turned.reshape(contexts, query_rows, heads * ROPE)
    packed = jnp.concatenate([weight, straight, turned], axis=1)

    def trade(array):
        return lax.ppermute(array, "tp", [(0, 1), (1, 0)])

    core = lax.axis_index("tp")
    turned_cache = latent_cache.T
    held = {0: lax.dynamic_slice_in_dim(turned_cache, core * half, half, 1)}
    for slot, source, bit in EARLY:
        held[slot] = swap(held[source], bit)
    waited = lax.optimization_barrier((packed, held[4], held[1], held[2], beside[1], beside[2]))
    packed, held[4], held[1], held[2], beside[1], beside[2] = waited
    packed = lax.all_to_all(packed, "ctx", 0, 0, tiled=True)
    for slot, source, bit in LATE:
        held[slot] = swap(held[source], bit)
    traded = {slot: trade(held[slot]) for slot in (1, 2)}
    waited = lax.optimization_barrier((packed, kept, held[3], held[5], held[6], traded))
    packed, kept, held[3], held[5], held[6], traded = waited
    others = lax.dynamic_slice_in_dim(packed, (me // near ^ 1) * near, near, 0)[:, :pair * depth]
    others = lax.ppermute(others, "groups", [(0, 1), (1, 0)])
    pieces = [turned_cache]
    for slot in range(1, contexts):
        if slot not in traded:
            traded[slot] = trade(held[slot])
        pieces += [held[slot], traded[slot]]

    query_count = contexts * query_rows
    on_chip = pl.BlockSpec(memory_space=pltpu.VMEM)
    scalars = pl.BlockSpec(memory_space=pltpu.SMEM)

    def attend(which, out_heads, operands):
        return pl.pallas_call(
            functools.partial(attend_kernel, contexts, pair, which),
            out_shape=jax.ShapeDtypeStruct((query_count, out_heads * VD), jnp.bfloat16),
            in_specs=[scalars, scalars] + [on_chip] * (len(operands) + len(pieces)),
            out_specs=on_chip,
            scratch_shapes=[pltpu.VMEM((contexts, pair * depth, width), jnp.bfloat16)] * which,
            compiler_params=pltpu.CompilerParams(vmem_limit_bytes=16 * 2**20),
            cost_estimate=pl.CostEstimate(flops=1 << 20, bytes_accessed=1 << 20, transcendentals=0),
            name="attend_" + ("first", "second")[which],
        )(block_order, span_start, *operands, *pieces)

    attended = attend(0, pair, [packed])
    attended = attend(1, heads, [packed, kept, *beside.values(), others, attended])
    attended = attended.reshape(contexts, query_rows, heads * VD)
    attended = lax.all_to_all(attended, "ctx", 0, 0, tiled=True)
    attended = attended.reshape(contexts, query_rows, heads, VD).transpose(1, 0, 2, 3)
    return attended.reshape(query_rows, head_count, VD)


def tile_update(running, tile_rows, tile_positions, gathered_queries, weight_matrix, query_last):
    row_max, row_total, accum = running
    softmax_scale = 1.0 / math.sqrt(NOPE + ROPE)
    head_count = gathered_queries.shape[1]
    latent = tile_rows[:, :LAT]
    rope_part = tile_rows[:, LAT:]
    key_value = jnp.dot(latent, weight_matrix, preferred_element_type=jnp.float32).astype(
        jnp.bfloat16
    )
    key_value = key_value.reshape(tile_rows.shape[0], head_count, NOPE + VD)
    scores = jnp.einsum(
        "qhc,khc->hqk",
        gathered_queries[:, :, :NOPE],
        key_value[:, :, :NOPE],
        preferred_element_type=jnp.float32,
    )
    scores = scores + jnp.einsum(
        "qhr,kr->hqk", gathered_queries[:, :, NOPE:], rope_part, preferred_element_type=jnp.float32
    )
    scores = scores * softmax_scale
    visible = (tile_positions[None, :] <= query_last[:, None])[None]
    scores = jnp.where(visible, scores, jnp.float32(-1e30))
    new_max = jnp.maximum(row_max, jnp.max(scores, axis=2))
    weights = jnp.where(visible, jnp.exp(scores - new_max[:, :, None]), jnp.float32(0.0))
    row_total = jnp.sum(weights, axis=2)
    accum = jnp.einsum(
        "hqk,khv->hqv",
        weights.astype(jnp.bfloat16),
        key_value[:, :, NOPE:],
        preferred_element_type=jnp.float32,
    )
    return (new_max, row_total, accum)


def split_by_context(queries, latent_cache, kv_weight, block_order, span_start):
    shard_index = lax.axis_index("ctx")
    gathered_queries = lax.all_gather(queries, "ctx", axis=0, tiled=True)
    full_weight = lax.all_gather(kv_weight, "ctx", axis=0, tiled=True)
    head_count = full_weight.shape[1]
    weight_matrix = full_weight.reshape(LAT, head_count * (NOPE + VD))
    row_count = latent_cache.shape[0]
    own_block = lax.dynamic_index_in_dim(block_order, shard_index, 0, keepdims=False)
    key_positions = own_block * row_count + jnp.arange(row_count, dtype=jnp.int32)
    query_count = gathered_queries.shape[0]
    query_last = span_start[0] + jnp.arange(query_count, dtype=jnp.int32)
    final_position = span_start[0] + query_count - 1
    running = (
        jnp.full((head_count, query_count), -1e30, jnp.float32),
        jnp.zeros((head_count, query_count), jnp.float32),
        jnp.zeros((head_count, query_count, VD), jnp.float32),
    )
    running = lax.cond(
        key_positions[0] <= final_position,
        lambda current, rows_now=latent_cache, places=key_positions: tile_update(
            current, rows_now, places, gathered_queries, weight_matrix, query_last
        ),
        lambda current: current,
        running,
    )
    row_max, row_total, accum = running
    parts_accum, parts_max, parts_total = (
        lax.all_to_all(
            accum[:, :, None, :].astype(jnp.bfloat16),
            "ctx",
            split_axis=1,
            concat_axis=2,
            tiled=True,
        ).astype(jnp.float32),
        lax.all_to_all(
            row_max[:, :, None].astype(jnp.bfloat16), "ctx", split_axis=1, concat_axis=2, tiled=True
        ).astype(jnp.float32),
        lax.all_to_all(
            row_total[:, :, None].astype(jnp.bfloat16),
            "ctx",
            split_axis=1,
            concat_axis=2,
            tiled=True,
        ).astype(jnp.float32),
    )
    overall = jnp.max(parts_max, axis=2, keepdims=True)
    factor = jnp.exp(parts_max - overall)
    denominator = jnp.sum(factor * parts_total, axis=2)
    numerator = jnp.sum(factor[:, :, :, None] * parts_accum, axis=2)
    result = (numerator / denominator[:, :, None]).astype(jnp.bfloat16)
    return jnp.transpose(result, (1, 0, 2))


def solution(mesh):
    contexts = mesh.shape["ctx"]
    cores = mesh.shape["tp"]

    def local(queries, latent_cache, kv_weight, block_order, span_start):
        arrays = (queries, latent_cache, kv_weight, block_order, span_start)
        paired = queries.shape[1] % (2 * contexts) == 0 and contexts == 1 + len(EARLY) + len(LATE)
        if paired and cores == 2 and mesh.shape["groups"] == 2:
            return split_by_heads(contexts, cores, *arrays)
        return split_by_context(*arrays)

    return jax.shard_map(
        local,
        mesh=mesh,
        in_specs=(
            P(("groups", "ctx"), "tp", None),
            P(("groups", "ctx"), None),
            P("ctx", "tp", None),
            P("groups"),
            P("groups"),
        ),
        out_specs=P(("groups", "ctx"), "tp", None),
        check_vma=False,
    )
```

```python
import functools
import math

import jax
import jax.numpy as jnp
from jax import lax
from jax.experimental import pallas as pl
from jax.experimental.pallas import tpu as pltpu
from jax.sharding import PartitionSpec as P

LAT = 512
ROPE = 64
NOPE = 128
VD = 128
HIDDEN = -1e30
EARLY = ((4, 0, 4), (1, 0, 1), (2, 0, 2))
LATE = ((3, 2, 1), (5, 4, 1), (6, 4, 2), (7, 5, 2))


def attend_kernel(slots, pair, which, *refs):
    me = lax.axis_index("ctx")
    order_ref, start_ref, packed_ref = refs[:3]
    if which == 0:
        weight_ref = packed_ref
        refs = refs[3:]
    else:
        near = slots // 2
        near_refs, (others_ref, done_ref) = refs[3:3 + near], refs[3 + near:5 + near]
        *refs, weight_ref = refs[5 + near:]
        for slot, near_ref in enumerate(near_refs):
            weight_ref[me ^ slot] = near_ref[...]
        weight_ref[pl.ds((me // near ^ 1) * near, near)] = others_ref[...]
    own_ref, *piece_refs, out_ref = refs
    core = lax.axis_index("tp")
    rows = own_ref.shape[1]
    half = rows // 2
    width = NOPE + VD
    depth = LAT // slots
    query_rows = (packed_ref.shape[1] - pair * depth) // 3
    query_count = slots * query_rows
    scale = math.log2(math.e) / math.sqrt(NOPE + ROPE)
    first = pair * depth
    weights, queries = [], []
    for member in range(pair):
        head = which * pair + member
        weights.append(weight_ref[:, member * depth:(member + 1) * depth, :].reshape(LAT, width))
        begin = first + which * query_rows
        part = packed_ref[:, begin:begin + query_rows, member * NOPE:(member + 1) * NOPE]
        part = part.reshape(query_count, NOPE)
        begin = first + 2 * query_rows
        turned = packed_ref[:, begin:begin + query_rows, head * ROPE:(head + 1) * ROPE]
        turned = turned.reshape(query_count, ROPE)
        queries.append(jnp.concatenate([part, turned], axis=1))
    weights = jnp.concatenate(weights, axis=1).T
    ahead = lax.broadcasted_iota(jnp.int32, (query_count, half), 1) - lax.broadcasted_iota(
        jnp.int32, (query_count, half), 0
    )
    scores = [[] for _ in range(pair)]
    values = [[] for _ in range(pair)]
    for base in range(0, slots, 4):
        parts, visible = [], []
        for slot in range(base, base + 4):
            places = (0, half)
            if slot > 0:
                places = (core * half, (1 - core) * half)
                parts += [piece_refs[2 * slot - 2][...], piece_refs[2 * slot - 1][...]]
            else:
                parts.append(own_ref[...])
            limit = start_ref[0] - order_ref[me ^ slot] * rows
            visible += [ahead <= limit - place for place in places]
        latent = jnp.concatenate(parts, axis=1)
        visible = jnp.concatenate(visible, axis=1)
        projected = jnp.dot(weights, latent[:LAT], preferred_element_type=jnp.float32)
        projected = projected.astype(jnp.bfloat16)
        rope = latent[LAT:]
        for member in range(pair):
            begin = member * width
            keys = jnp.concatenate(
                [projected[begin:begin + NOPE], rope], axis=0
            )
            score = jnp.dot(queries[member], keys, preferred_element_type=jnp.float32)
            scores[member].append(jnp.where(visible, score, HIDDEN))
            values[member].append(projected[begin + NOPE:begin + width])
    results = []
    for member in range(pair):
        score = jnp.concatenate(scores[member], axis=1)
        top = jnp.max(score, axis=1, keepdims=True)
        probs = jnp.exp2((score - top) * scale)
        totals = jnp.sum(probs, axis=1, keepdims=True)
        result = lax.dot_general(
            probs.astype(jnp.bfloat16), jnp.concatenate(values[member], axis=1),
            (((1,), (1,)), ((), ())), preferred_element_type=jnp.float32,
        )
        results.append((result / totals).astype(jnp.bfloat16))
    place = 0
    if which == 1:
        group = lax.axis_index("groups")
        out_ref[:, pl.ds(pl.multiple_of(group * pair * VD, pair * VD), pair * VD)] = done_ref[...]
        place = pl.multiple_of((1 - group) * pair * VD, pair * VD)
    out_ref[:, pl.ds(place, pair * VD)] = jnp.concatenate(results, axis=1)


def split_by_heads(contexts, cores, queries, latent_cache, kv_weight, block_order, span_start):
    query_rows, head_count, query_width = queries.shape
    heads = head_count // contexts
    pair = heads // 2
    rows = latent_cache.shape[0]
    half = rows // cores
    depth = kv_weight.shape[0]
    width = NOPE + VD
    group = lax.axis_index("groups")

    def swap(array, bit):
        return lax.ppermute(array, "ctx", [(i, i ^ bit) for i in range(contexts)])

    me = lax.axis_index("ctx")
    by_head = kv_weight.reshape(depth, contexts, 2, pair, width)
    weight = lax.dynamic_index_in_dim(by_head, group, 2, keepdims=False)
    weight = weight.transpose(1, 2, 0, 3).reshape(contexts, pair * depth, width)

    def second_pair(owner):
        part = lax.dynamic_slice(
            by_head, (0, owner, 1 - group, 0, 0), (depth, 1, 1, pair, width)
        )
        part = part.reshape(depth, pair, width).transpose(1, 0, 2)
        return part.reshape(pair * depth, width)

    kept = second_pair(me)
    near = contexts // 2
    beside = {slot: swap(second_pair(me ^ slot), slot) for slot in range(1, near)}
    query = queries.reshape(query_rows, contexts, 2, pair, query_width)
    query = jnp.where(group == 0, query, query[:, :, ::-1])
    straight = query[..., :NOPE].transpose(1, 2, 0, 3, 4)
    straight = straight.reshape(contexts, 2 * query_rows, pair * NOPE)
    turned = query[..., NOPE:].transpose(1, 0, 2, 3, 4)
    turned = turned.reshape(contexts, query_rows, heads * ROPE)
    packed = jnp.concatenate([weight, straight, turned], axis=1)

    def trade(array):
        return lax.ppermute(array, "tp", [(0, 1), (1, 0)])

    core = lax.axis_index("tp")
    turned_cache = latent_cache.T
    held = {0: lax.dynamic_slice_in_dim(turned_cache, core * half, half, 1)}
    for slot, source, bit in EARLY:
        held[slot] = swap(held[source], bit)
    waited = lax.optimization_barrier((packed, held[4], held[1], held[2], beside[1], beside[2]))
    packed, held[4], held[1], held[2], beside[1], beside[2] = waited
    packed = lax.all_to_all(packed, "ctx", 0, 0, tiled=True)
    for slot, source, bit in LATE:
        held[slot] = swap(held[source], bit)
    traded = {slot: trade(held[slot]) for slot in (1, 2)}
    waited = lax.optimization_barrier((packed, kept, held[3], held[5], held[6], traded))
    packed, kept, held[3], held[5], held[6], traded = waited
    others = lax.dynamic_slice_in_dim(packed, (me // near ^ 1) * near, near, 0)[:, :pair * depth]
    others = lax.ppermute(others, "groups", [(0, 1), (1, 0)])
    pieces = [turned_cache]
    for slot in range(1, contexts):
        if slot not in traded:
            traded[slot] = trade(held[slot])
        pieces += [held[slot], traded[slot]]

    query_count = contexts * query_rows
    on_chip = pl.BlockSpec(memory_space=pltpu.VMEM)
    scalars = pl.BlockSpec(memory_space=pltpu.SMEM)

    def attend(which, out_heads, operands):
        return pl.pallas_call(
            functools.partial(attend_kernel, contexts, pair, which),
            out_shape=jax.ShapeDtypeStruct((query_count, out_heads * VD), jnp.bfloat16),
            in_specs=[scalars, scalars] + [on_chip] * (len(operands) + len(pieces)),
            out_specs=on_chip,
            scratch_shapes=[pltpu.VMEM((contexts, pair * depth, width), jnp.bfloat16)] * which,
            compiler_params=pltpu.CompilerParams(vmem_limit_bytes=16 * 2**20),
            cost_estimate=pl.CostEstimate(flops=1 << 20, bytes_accessed=1 << 20, transcendentals=0),
            name="attend_" + ("first", "second")[which],
        )(block_order, span_start, *operands, *pieces)

    attended = attend(0, pair, [packed])
    attended = attend(1, heads, [packed, kept, *beside.values(), others, attended])
    attended = attended.reshape(contexts, query_rows, heads * VD)
    attended = lax.all_to_all(attended, "ctx", 0, 0, tiled=True)
    attended = attended.reshape(contexts, query_rows, heads, VD).transpose(1, 0, 2, 3)
    return attended.reshape(query_rows, head_count, VD)


def tile_update(running, tile_rows, tile_positions, gathered_queries, weight_matrix, query_last):
    row_max, row_total, accum = running
    softmax_scale = 1.0 / math.sqrt(NOPE + ROPE)
    head_count = gathered_queries.shape[1]
    latent = tile_rows[:, :LAT]
    rope_part = tile_rows[:, LAT:]
    key_value = jnp.dot(latent, weight_matrix, preferred_element_type=jnp.float32).astype(
        jnp.bfloat16
    )
    key_value = key_value.reshape(tile_rows.shape[0], head_count, NOPE + VD)
    scores = jnp.einsum(
        "qhc,khc->hqk",
        gathered_queries[:, :, :NOPE],
        key_value[:, :, :NOPE],
        preferred_element_type=jnp.float32,
    )
    scores = scores + jnp.einsum(
        "qhr,kr->hqk", gathered_queries[:, :, NOPE:], rope_part, preferred_element_type=jnp.float32
    )
    scores = scores * softmax_scale
    visible = (tile_positions[None, :] <= query_last[:, None])[None]
    scores = jnp.where(visible, scores, jnp.float32(-1e30))
    new_max = jnp.maximum(row_max, jnp.max(scores, axis=2))
    weights = jnp.where(visible, jnp.exp(scores - new_max[:, :, None]), jnp.float32(0.0))
    row_total = jnp.sum(weights, axis=2)
    accum = jnp.einsum(
        "hqk,khv->hqv",
        weights.astype(jnp.bfloat16),
        key_value[:, :, NOPE:],
        preferred_element_type=jnp.float32,
    )
    return (new_max, row_total, accum)


def split_by_context(queries, latent_cache, kv_weight, block_order, span_start):
    shard_index = lax.axis_index("ctx")
    gathered_queries = lax.all_gather(queries, "ctx", axis=0, tiled=True)
    full_weight = lax.all_gather(kv_weight, "ctx", axis=0, tiled=True)
    head_count = full_weight.shape[1]
    weight_matrix = full_weight.reshape(LAT, head_count * (NOPE + VD))
    row_count = latent_cache.shape[0]
    own_block = lax.dynamic_index_in_dim(block_order, shard_index, 0, keepdims=False)
    key_positions = own_block * row_count + jnp.arange(row_count, dtype=jnp.int32)
    query_count = gathered_queries.shape[0]
    query_last = span_start[0] + jnp.arange(query_count, dtype=jnp.int32)
    final_position = span_start[0] + query_count - 1
    running = (
        jnp.full((head_count, query_count), -1e30, jnp.float32),
        jnp.zeros((head_count, query_count), jnp.float32),
        jnp.zeros((head_count, query_count, VD), jnp.float32),
    )
    running = lax.cond(
        key_positions[0] <= final_position,
        lambda current, rows_now=latent_cache, places=key_positions: tile_update(
            current, rows_now, places, gathered_queries, weight_matrix, query_last
        ),
        lambda current: current,
        running,
    )
    row_max, row_total, accum = running
    parts_accum, parts_max, parts_total = (
        lax.all_to_all(
            accum[:, :, None, :].astype(jnp.bfloat16),
            "ctx",
            split_axis=1,
            concat_axis=2,
            tiled=True,
        ).astype(jnp.float32),
        lax.all_to_all(
            row_max[:, :, None].astype(jnp.bfloat16), "ctx", split_axis=1, concat_axis=2, tiled=True
        ).astype(jnp.float32),
        lax.all_to_all(
            row_total[:, :, None].astype(jnp.bfloat16),
            "ctx",
            split_axis=1,
            concat_axis=2,
            tiled=True,
        ).astype(jnp.float32),
    )
    overall = jnp.max(parts_max, axis=2, keepdims=True)
    factor = jnp.exp(parts_max - overall)
    denominator = jnp.sum(factor * parts_total, axis=2)
    numerator = jnp.sum(factor[:, :, :, None] * parts_accum, axis=2)
    result = (numerator / denominator[:, :, None]).astype(jnp.bfloat16)
    return jnp.transpose(result, (1, 0, 2))


def solution(mesh):
    contexts = mesh.shape["ctx"]
    cores = mesh.shape["tp"]

    def local(queries, latent_cache, kv_weight, block_order, span_start):
        arrays = (queries, latent_cache, kv_weight, block_order, span_start)
        paired = queries.shape[1] % (2 * contexts) == 0 and contexts == 1 + len(EARLY) + len(LATE)
        if paired and cores == 2 and mesh.shape["groups"] == 2:
            return split_by_heads(contexts, cores, *arrays)
        return split_by_context(*arrays)

    return jax.shard_map(
        local,
        mesh=mesh,
        in_specs=(
            P(("groups", "ctx"), "tp", None),
            P(("groups", "ctx"), None),
            P("ctx", "tp", None),
            P("groups"),
            P("groups"),
        ),
        out_specs=P(("groups", "ctx"), "tp", None),
        check_vma=False,
    )
```

```python
import functools
import math

import jax
import jax.numpy as jnp
from jax import lax
from jax.experimental import pallas as pl
from jax.experimental.pallas import tpu as pltpu
from jax.sharding import PartitionSpec as P

LAT = 512
ROPE = 64
NOPE = 128
VD = 128
HIDDEN = -1e30
EARLY = ((4, 0, 4), (1, 0, 1), (2, 0, 2))
LATE = ((3, 2, 1), (5, 4, 1), (6, 4, 2), (7, 5, 2))


def attend_kernel(slots, pair, which, *refs):
    me = lax.axis_index("ctx")
    order_ref, start_ref, packed_ref = refs[:3]
    if which == 0:
        weight_ref = packed_ref
        refs = refs[3:]
    else:
        near = slots // 2
        near_refs, (others_ref, done_ref) = refs[3:3 + near], refs[3 + near:5 + near]
        *refs, weight_ref = refs[5 + near:]
        for slot, near_ref in enumerate(near_refs):
            weight_ref[me ^ slot] = near_ref[...]
        weight_ref[pl.ds((me // near ^ 1) * near, near)] = others_ref[...]
    own_ref, *piece_refs, out_ref = refs
    core = lax.axis_index("tp")
    rows = own_ref.shape[1]
    half = rows // 2
    width = NOPE + VD
    depth = LAT // slots
    query_rows = (packed_ref.shape[1] - pair * depth) // 3
    query_count = slots * query_rows
    scale = math.log2(math.e) / math.sqrt(NOPE + ROPE)
    first = pair * depth
    weights, queries = [], []
    for member in range(pair):
        head = which * pair + member
        weights.append(weight_ref[:, member * depth:(member + 1) * depth, :].reshape(LAT, width))
        begin = first + which * query_rows
        part = packed_ref[:, begin:begin + query_rows, member * NOPE:(member + 1) * NOPE]
        part = part.reshape(query_count, NOPE)
        begin = first + 2 * query_rows
        turned = packed_ref[:, begin:begin + query_rows, head * ROPE:(head + 1) * ROPE]
        turned = turned.reshape(query_count, ROPE)
        queries.append(jnp.concatenate([part, turned], axis=1))
    weights = jnp.concatenate(weights, axis=1).T
    ahead = lax.broadcasted_iota(jnp.int32, (query_count, half), 1) - lax.broadcasted_iota(
        jnp.int32, (query_count, half), 0
    )
    scores = [[] for _ in range(pair)]
    values = [[] for _ in range(pair)]
    for base in range(0, slots, 4):
        parts, visible = [], []
        for slot in range(base, base + 4):
            places = (0, half)
            if slot > 0:
                places = (core * half, (1 - core) * half)
                parts += [piece_refs[2 * slot - 2][...], piece_refs[2 * slot - 1][...]]
            else:
                parts.append(own_ref[...])
            limit = start_ref[0] - order_ref[me ^ slot] * rows
            visible += [ahead <= limit - place for place in places]
        latent = jnp.concatenate(parts, axis=1)
        visible = jnp.concatenate(visible, axis=1)
        projected = jnp.dot(weights, latent[:LAT], preferred_element_type=jnp.float32)
        projected = projected.astype(jnp.bfloat16)
        rope = latent[LAT:]
        for member in range(pair):
            begin = member * width
            keys = jnp.concatenate(
                [projected[begin:begin + NOPE], rope], axis=0
            )
            score = jnp.dot(queries[member], keys, preferred_element_type=jnp.float32)
            scores[member].append(jnp.where(visible, score, HIDDEN))
            values[member].append(projected[begin + NOPE:begin + width])
    results = []
    for member in range(pair):
        score = jnp.concatenate(scores[member], axis=1)
        top = jnp.max(score, axis=1, keepdims=True)
        probs = jnp.exp2((score - top) * scale)
        totals = jnp.sum(probs, axis=1, keepdims=True)
        result = lax.dot_general(
            probs.astype(jnp.bfloat16), jnp.concatenate(values[member], axis=1),
            (((1,), (1,)), ((), ())), preferred_element_type=jnp.float32,
        )
        results.append((result / totals).astype(jnp.bfloat16))
    place = 0
    if which == 1:
        group = lax.axis_index("groups")
        out_ref[:, pl.ds(pl.multiple_of(group * pair * VD, pair * VD), pair * VD)] = done_ref[...]
        place = pl.multiple_of((1 - group) * pair * VD, pair * VD)
    out_ref[:, pl.ds(place, pair * VD)] = jnp.concatenate(results, axis=1)


def split_by_heads(contexts, cores, queries, latent_cache, kv_weight, block_order, span_start):
    query_rows, head_count, query_width = queries.shape
    heads = head_count // contexts
    pair = heads // 2
    rows = latent_cache.shape[0]
    half = rows // cores
    depth = kv_weight.shape[0]
    width = NOPE + VD
    group = lax.axis_index("groups")

    def swap(array, bit):
        return lax.ppermute(array, "ctx", [(i, i ^ bit) for i in range(contexts)])

    me = lax.axis_index("ctx")
    by_head = kv_weight.reshape(depth, contexts, 2, pair, width)
    weight = lax.dynamic_index_in_dim(by_head, group, 2, keepdims=False)
    weight = weight.transpose(1, 2, 0, 3).reshape(contexts, pair * depth, width)

    def second_pair(owner):
        part = lax.dynamic_slice(
            by_head, (0, owner, 1 - group, 0, 0), (depth, 1, 1, pair, width)
        )
        part = part.reshape(depth, pair, width).transpose(1, 0, 2)
        return part.reshape(pair * depth, width)

    kept = second_pair(me)
    near = contexts // 2
    beside = {slot: swap(second_pair(me ^ slot), slot) for slot in range(1, near)}
    query = queries.reshape(query_rows, contexts, 2, pair, query_width)
    query = jnp.where(group == 0, query, query[:, :, ::-1])
    straight = query[..., :NOPE].transpose(1, 2, 0, 3, 4)
    straight = straight.reshape(contexts, 2 * query_rows, pair * NOPE)
    turned = query[..., NOPE:].transpose(1, 0, 2, 3, 4)
    turned = turned.reshape(contexts, query_rows, heads * ROPE)
    packed = jnp.concatenate([weight, straight, turned], axis=1)

    def trade(array):
        return lax.ppermute(array, "tp", [(0, 1), (1, 0)])

    core = lax.axis_index("tp")
    turned_cache = latent_cache.T
    held = {0: lax.dynamic_slice_in_dim(turned_cache, core * half, half, 1)}
    for slot, source, bit in EARLY:
        held[slot] = swap(held[source], bit)
    waited = lax.optimization_barrier((packed, held[4], held[1], held[2], beside[1], beside[2]))
    packed, held[4], held[1], held[2], beside[1], beside[2] = waited
    packed = lax.all_to_all(packed, "ctx", 0, 0, tiled=True)
    for slot, source, bit in LATE:
        held[slot] = swap(held[source], bit)
    traded = {slot: trade(held[slot]) for slot in (1, 2, 3)}
    waited = lax.optimization_barrier((packed, kept, held[3], held[5], held[6], traded))
    packed, kept, held[3], held[5], held[6], traded = waited
    others = lax.dynamic_slice_in_dim(packed, (me // near ^ 1) * near, near, 0)[:, :pair * depth]
    others = lax.ppermute(others, "groups", [(0, 1), (1, 0)])
    pieces = [turned_cache]
    for slot in range(1, contexts):
        if slot not in traded:
            traded[slot] = trade(held[slot])
        pieces += [held[slot], traded[slot]]

    query_count = contexts * query_rows
    on_chip = pl.BlockSpec(memory_space=pltpu.VMEM)
    scalars = pl.BlockSpec(memory_space=pltpu.SMEM)

    def attend(which, out_heads, operands):
        return pl.pallas_call(
            functools.partial(attend_kernel, contexts, pair, which),
            out_shape=jax.ShapeDtypeStruct((query_count, out_heads * VD), jnp.bfloat16),
            in_specs=[scalars, scalars] + [on_chip] * (len(operands) + len(pieces)),
            out_specs=on_chip,
            scratch_shapes=[pltpu.VMEM((contexts, pair * depth, width), jnp.bfloat16)] * which,
            compiler_params=pltpu.CompilerParams(vmem_limit_bytes=16 * 2**20),
            cost_estimate=pl.CostEstimate(flops=1 << 20, bytes_accessed=1 << 20, transcendentals=0),
            name="attend_" + ("first", "second")[which],
        )(block_order, span_start, *operands, *pieces)

    attended = attend(0, pair, [packed])
    attended = attend(1, heads, [packed, kept, *beside.values(), others, attended])
    attended = attended.reshape(contexts, query_rows, heads * VD)
    attended = lax.all_to_all(attended, "ctx", 0, 0, tiled=True)
    attended = attended.reshape(contexts, query_rows, heads, VD).transpose(1, 0, 2, 3)
    return attended.reshape(query_rows, head_count, VD)


def tile_update(running, tile_rows, tile_positions, gathered_queries, weight_matrix, query_last):
    row_max, row_total, accum = running
    softmax_scale = 1.0 / math.sqrt(NOPE + ROPE)
    head_count = gathered_queries.shape[1]
    latent = tile_rows[:, :LAT]
    rope_part = tile_rows[:, LAT:]
    key_value = jnp.dot(latent, weight_matrix, preferred_element_type=jnp.float32).astype(
        jnp.bfloat16
    )
    key_value = key_value.reshape(tile_rows.shape[0], head_count, NOPE + VD)
    scores = jnp.einsum(
        "qhc,khc->hqk",
        gathered_queries[:, :, :NOPE],
        key_value[:, :, :NOPE],
        preferred_element_type=jnp.float32,
    )
    scores = scores + jnp.einsum(
        "qhr,kr->hqk", gathered_queries[:, :, NOPE:], rope_part, preferred_element_type=jnp.float32
    )
    scores = scores * softmax_scale
    visible = (tile_positions[None, :] <= query_last[:, None])[None]
    scores = jnp.where(visible, scores, jnp.float32(-1e30))
    new_max = jnp.maximum(row_max, jnp.max(scores, axis=2))
    weights = jnp.where(visible, jnp.exp(scores - new_max[:, :, None]), jnp.float32(0.0))
    row_total = jnp.sum(weights, axis=2)
    accum = jnp.einsum(
        "hqk,khv->hqv",
        weights.astype(jnp.bfloat16),
        key_value[:, :, NOPE:],
        preferred_element_type=jnp.float32,
    )
    return (new_max, row_total, accum)


def split_by_context(queries, latent_cache, kv_weight, block_order, span_start):
    shard_index = lax.axis_index("ctx")
    gathered_queries = lax.all_gather(queries, "ctx", axis=0, tiled=True)
    full_weight = lax.all_gather(kv_weight, "ctx", axis=0, tiled=True)
    head_count = full_weight.shape[1]
    weight_matrix = full_weight.reshape(LAT, head_count * (NOPE + VD))
    row_count = latent_cache.shape[0]
    own_block = lax.dynamic_index_in_dim(block_order, shard_index, 0, keepdims=False)
    key_positions = own_block * row_count + jnp.arange(row_count, dtype=jnp.int32)
    query_count = gathered_queries.shape[0]
    query_last = span_start[0] + jnp.arange(query_count, dtype=jnp.int32)
    final_position = span_start[0] + query_count - 1
    running = (
        jnp.full((head_count, query_count), -1e30, jnp.float32),
        jnp.zeros((head_count, query_count), jnp.float32),
        jnp.zeros((head_count, query_count, VD), jnp.float32),
    )
    running = lax.cond(
        key_positions[0] <= final_position,
        lambda current, rows_now=latent_cache, places=key_positions: tile_update(
            current, rows_now, places, gathered_queries, weight_matrix, query_last
        ),
        lambda current: current,
        running,
    )
    row_max, row_total, accum = running
    parts_accum, parts_max, parts_total = (
        lax.all_to_all(
            accum[:, :, None, :].astype(jnp.bfloat16),
            "ctx",
            split_axis=1,
            concat_axis=2,
            tiled=True,
        ).astype(jnp.float32),
        lax.all_to_all(
            row_max[:, :, None].astype(jnp.bfloat16), "ctx", split_axis=1, concat_axis=2, tiled=True
        ).astype(jnp.float32),
        lax.all_to_all(
            row_total[:, :, None].astype(jnp.bfloat16),
            "ctx",
            split_axis=1,
            concat_axis=2,
            tiled=True,
        ).astype(jnp.float32),
    )
    overall = jnp.max(parts_max, axis=2, keepdims=True)
    factor = jnp.exp(parts_max - overall)
    denominator = jnp.sum(factor * parts_total, axis=2)
    numerator = jnp.sum(factor[:, :, :, None] * parts_accum, axis=2)
    result = (numerator / denominator[:, :, None]).astype(jnp.bfloat16)
    return jnp.transpose(result, (1, 0, 2))


def solution(mesh):
    contexts = mesh.shape["ctx"]
    cores = mesh.shape["tp"]

    def local(queries, latent_cache, kv_weight, block_order, span_start):
        arrays = (queries, latent_cache, kv_weight, block_order, span_start)
        paired = queries.shape[1] % (2 * contexts) == 0 and contexts == 1 + len(EARLY) + len(LATE)
        if paired and cores == 2 and mesh.shape["groups"] == 2:
            return split_by_heads(contexts, cores, *arrays)
        return split_by_context(*arrays)

    return jax.shard_map(
        local,
        mesh=mesh,
        in_specs=(
            P(("groups", "ctx"), "tp", None),
            P(("groups", "ctx"), None),
            P("ctx", "tp", None),
            P("groups"),
            P("groups"),
        ),
        out_specs=P(("groups", "ctx"), "tp", None),
        check_vma=False,
    )
```

```python
import functools
import math

import jax
import jax.numpy as jnp
from jax import lax
from jax.experimental import pallas as pl
from jax.experimental.pallas import tpu as pltpu
from jax.sharding import PartitionSpec as P

LAT = 512
ROPE = 64
NOPE = 128
VD = 128
HIDDEN = -1e30
EARLY = ((4, 0, 4), (1, 0, 1), (2, 0, 2))
LATE = ((3, 2, 1), (5, 4, 1), (6, 4, 2), (7, 6, 1))


def attend_kernel(slots, pair, which, *refs):
    me = lax.axis_index("ctx")
    order_ref, start_ref, packed_ref = refs[:3]
    if which == 0:
        weight_ref = packed_ref
        refs = refs[3:]
    else:
        near = slots // 2
        near_refs, (others_ref, done_ref) = refs[3:3 + near], refs[3 + near:5 + near]
        *refs, weight_ref = refs[5 + near:]
        for slot, near_ref in enumerate(near_refs):
            weight_ref[me ^ slot] = near_ref[...]
        weight_ref[pl.ds((me // near ^ 1) * near, near)] = others_ref[...]
    own_ref, *piece_refs, out_ref = refs
    core = lax.axis_index("tp")
    rows = own_ref.shape[1]
    half = rows // 2
    width = NOPE + VD
    depth = LAT // slots
    query_rows = (packed_ref.shape[1] - pair * depth) // 3
    query_count = slots * query_rows
    scale = math.log2(math.e) / math.sqrt(NOPE + ROPE)
    first = pair * depth
    weights, queries = [], []
    for member in range(pair):
        head = which * pair + member
        weights.append(weight_ref[:, member * depth:(member + 1) * depth, :].reshape(LAT, width))
        begin = first + which * query_rows
        part = packed_ref[:, begin:begin + query_rows, member * NOPE:(member + 1) * NOPE]
        part = part.reshape(query_count, NOPE)
        begin = first + 2 * query_rows
        turned = packed_ref[:, begin:begin + query_rows, head * ROPE:(head + 1) * ROPE]
        turned = turned.reshape(query_count, ROPE)
        queries.append(jnp.concatenate([part, turned], axis=1))
    weights = jnp.concatenate(weights, axis=1).T
    ahead = lax.broadcasted_iota(jnp.int32, (query_count, half), 1) - lax.broadcasted_iota(
        jnp.int32, (query_count, half), 0
    )
    scores = [[] for _ in range(pair)]
    values = [[] for _ in range(pair)]
    for base in range(0, slots, 4):
        parts, visible = [], []
        for slot in range(base, base + 4):
            places = (0, half)
            if slot > 0:
                places = (core * half, (1 - core) * half)
                parts += [piece_refs[2 * slot - 2][...], piece_refs[2 * slot - 1][...]]
            else:
                parts.append(own_ref[...])
            limit = start_ref[0] - order_ref[me ^ slot] * rows
            visible += [ahead <= limit - place for place in places]
        latent = jnp.concatenate(parts, axis=1)
        visible = jnp.concatenate(visible, axis=1)
        projected = jnp.dot(weights, latent[:LAT], preferred_element_type=jnp.float32)
        projected = projected.astype(jnp.bfloat16)
        rope = latent[LAT:]
        for member in range(pair):
            begin = member * width
            keys = jnp.concatenate(
                [projected[begin:begin + NOPE], rope], axis=0
            )
            score = jnp.dot(queries[member], keys, preferred_element_type=jnp.float32)
            scores[member].append(jnp.where(visible, score, HIDDEN))
            values[member].append(projected[begin + NOPE:begin + width])
    results = []
    for member in range(pair):
        score = jnp.concatenate(scores[member], axis=1)
        top = jnp.max(score, axis=1, keepdims=True)
        probs = jnp.exp2((score - top) * scale)
        totals = jnp.sum(probs, axis=1, keepdims=True)
        result = lax.dot_general(
            probs.astype(jnp.bfloat16), jnp.concatenate(values[member], axis=1),
            (((1,), (1,)), ((), ())), preferred_element_type=jnp.float32,
        )
        results.append((result / totals).astype(jnp.bfloat16))
    place = 0
    if which == 1:
        group = lax.axis_index("groups")
        out_ref[:, pl.ds(pl.multiple_of(group * pair * VD, pair * VD), pair * VD)] = done_ref[...]
        place = pl.multiple_of((1 - group) * pair * VD, pair * VD)
    out_ref[:, pl.ds(place, pair * VD)] = jnp.concatenate(results, axis=1)


def split_by_heads(contexts, cores, queries, latent_cache, kv_weight, block_order, span_start):
    query_rows, head_count, query_width = queries.shape
    heads = head_count // contexts
    pair = heads // 2
    rows = latent_cache.shape[0]
    half = rows // cores
    depth = kv_weight.shape[0]
    width = NOPE + VD
    group = lax.axis_index("groups")

    def swap(array, bit):
        return lax.ppermute(array, "ctx", [(i, i ^ bit) for i in range(contexts)])

    me = lax.axis_index("ctx")
    by_head = kv_weight.reshape(depth, contexts, 2, pair, width)
    weight = lax.dynamic_index_in_dim(by_head, group, 2, keepdims=False)
    weight = weight.transpose(1, 2, 0, 3).reshape(contexts, pair * depth, width)

    def second_pair(owner):
        part = lax.dynamic_slice(
            by_head, (0, owner, 1 - group, 0, 0), (depth, 1, 1, pair, width)
        )
        part = part.reshape(depth, pair, width).transpose(1, 0, 2)
        return part.reshape(pair * depth, width)

    kept = second_pair(me)
    near = contexts // 2
    beside = {slot: swap(second_pair(me ^ slot), slot) for slot in range(1, near)}
    query = queries.reshape(query_rows, contexts, 2, pair, query_width)
    query = jnp.where(group == 0, query, query[:, :, ::-1])
    straight = query[..., :NOPE].transpose(1, 2, 0, 3, 4)
    straight = straight.reshape(contexts, 2 * query_rows, pair * NOPE)
    turned = query[..., NOPE:].transpose(1, 0, 2, 3, 4)
    turned = turned.reshape(contexts, query_rows, heads * ROPE)
    packed = jnp.concatenate([weight, straight, turned], axis=1)

    def trade(array):
        return lax.ppermute(array, "tp", [(0, 1), (1, 0)])

    core = lax.axis_index("tp")
    turned_cache = latent_cache.T
    held = {0: lax.dynamic_slice_in_dim(turned_cache, core * half, half, 1)}
    for slot, source, bit in EARLY:
        held[slot] = swap(held[source], bit)
    waited = lax.optimization_barrier((packed, held[4], held[1], held[2], beside[1], beside[2]))
    packed, held[4], held[1], held[2], beside[1], beside[2] = waited
    packed = lax.all_to_all(packed, "ctx", 0, 0, tiled=True)
    for slot, source, bit in LATE:
        held[slot] = swap(held[source], bit)
    traded = {slot: trade(held[slot]) for slot in (1, 2, 3)}
    waited = lax.optimization_barrier((packed, kept, held[3], held[5], held[6], traded))
    packed, kept, held[3], held[5], held[6], traded = waited
    others = lax.dynamic_slice_in_dim(packed, (me // near ^ 1) * near, near, 0)[:, :pair * depth]
    others = lax.ppermute(others, "groups", [(0, 1), (1, 0)])
    pieces = [turned_cache]
    for slot in range(1, contexts):
        if slot not in traded:
            traded[slot] = trade(held[slot])
        pieces += [held[slot], traded[slot]]

    query_count = contexts * query_rows
    on_chip = pl.BlockSpec(memory_space=pltpu.VMEM)
    scalars = pl.BlockSpec(memory_space=pltpu.SMEM)

    def attend(which, out_heads, operands):
        return pl.pallas_call(
            functools.partial(attend_kernel, contexts, pair, which),
            out_shape=jax.ShapeDtypeStruct((query_count, out_heads * VD), jnp.bfloat16),
            in_specs=[scalars, scalars] + [on_chip] * (len(operands) + len(pieces)),
            out_specs=on_chip,
            scratch_shapes=[pltpu.VMEM((contexts, pair * depth, width), jnp.bfloat16)] * which,
            compiler_params=pltpu.CompilerParams(vmem_limit_bytes=16 * 2**20),
            cost_estimate=pl.CostEstimate(flops=1 << 20, bytes_accessed=1 << 20, transcendentals=0),
            name="attend_" + ("first", "second")[which],
        )(block_order, span_start, *operands, *pieces)

    attended = attend(0, pair, [packed])
    attended = attend(1, heads, [packed, kept, *beside.values(), others, attended])
    attended = attended.reshape(contexts, query_rows, heads * VD)
    attended = lax.all_to_all(attended, "ctx", 0, 0, tiled=True)
    attended = attended.reshape(contexts, query_rows, heads, VD).transpose(1, 0, 2, 3)
    return attended.reshape(query_rows, head_count, VD)


def tile_update(running, tile_rows, tile_positions, gathered_queries, weight_matrix, query_last):
    row_max, row_total, accum = running
    softmax_scale = 1.0 / math.sqrt(NOPE + ROPE)
    head_count = gathered_queries.shape[1]
    latent = tile_rows[:, :LAT]
    rope_part = tile_rows[:, LAT:]
    key_value = jnp.dot(latent, weight_matrix, preferred_element_type=jnp.float32).astype(
        jnp.bfloat16
    )
    key_value = key_value.reshape(tile_rows.shape[0], head_count, NOPE + VD)
    scores = jnp.einsum(
        "qhc,khc->hqk",
        gathered_queries[:, :, :NOPE],
        key_value[:, :, :NOPE],
        preferred_element_type=jnp.float32,
    )
    scores = scores + jnp.einsum(
        "qhr,kr->hqk", gathered_queries[:, :, NOPE:], rope_part, preferred_element_type=jnp.float32
    )
    scores = scores * softmax_scale
    visible = (tile_positions[None, :] <= query_last[:, None])[None]
    scores = jnp.where(visible, scores, jnp.float32(-1e30))
    new_max = jnp.maximum(row_max, jnp.max(scores, axis=2))
    weights = jnp.where(visible, jnp.exp(scores - new_max[:, :, None]), jnp.float32(0.0))
    row_total = jnp.sum(weights, axis=2)
    accum = jnp.einsum(
        "hqk,khv->hqv",
        weights.astype(jnp.bfloat16),
        key_value[:, :, NOPE:],
        preferred_element_type=jnp.float32,
    )
    return (new_max, row_total, accum)


def split_by_context(queries, latent_cache, kv_weight, block_order, span_start):
    shard_index = lax.axis_index("ctx")
    gathered_queries = lax.all_gather(queries, "ctx", axis=0, tiled=True)
    full_weight = lax.all_gather(kv_weight, "ctx", axis=0, tiled=True)
    head_count = full_weight.shape[1]
    weight_matrix = full_weight.reshape(LAT, head_count * (NOPE + VD))
    row_count = latent_cache.shape[0]
    own_block = lax.dynamic_index_in_dim(block_order, shard_index, 0, keepdims=False)
    key_positions = own_block * row_count + jnp.arange(row_count, dtype=jnp.int32)
    query_count = gathered_queries.shape[0]
    query_last = span_start[0] + jnp.arange(query_count, dtype=jnp.int32)
    final_position = span_start[0] + query_count - 1
    running = (
        jnp.full((head_count, query_count), -1e30, jnp.float32),
        jnp.zeros((head_count, query_count), jnp.float32),
        jnp.zeros((head_count, query_count, VD), jnp.float32),
    )
    running = lax.cond(
        key_positions[0] <= final_position,
        lambda current, rows_now=latent_cache, places=key_positions: tile_update(
            current, rows_now, places, gathered_queries, weight_matrix, query_last
        ),
        lambda current: current,
        running,
    )
    row_max, row_total, accum = running
    parts_accum, parts_max, parts_total = (
        lax.all_to_all(
            accum[:, :, None, :].astype(jnp.bfloat16),
            "ctx",
            split_axis=1,
            concat_axis=2,
            tiled=True,
        ).astype(jnp.float32),
        lax.all_to_all(
            row_max[:, :, None].astype(jnp.bfloat16), "ctx", split_axis=1, concat_axis=2, tiled=True
        ).astype(jnp.float32),
        lax.all_to_all(
            row_total[:, :, None].astype(jnp.bfloat16),
            "ctx",
            split_axis=1,
            concat_axis=2,
            tiled=True,
        ).astype(jnp.float32),
    )
    overall = jnp.max(parts_max, axis=2, keepdims=True)
    factor = jnp.exp(parts_max - overall)
    denominator = jnp.sum(factor * parts_total, axis=2)
    numerator = jnp.sum(factor[:, :, :, None] * parts_accum, axis=2)
    result = (numerator / denominator[:, :, None]).astype(jnp.bfloat16)
    return jnp.transpose(result, (1, 0, 2))


def solution(mesh):
    contexts = mesh.shape["ctx"]
    cores = mesh.shape["tp"]

    def local(queries, latent_cache, kv_weight, block_order, span_start):
        arrays = (queries, latent_cache, kv_weight, block_order, span_start)
        paired = queries.shape[1] % (2 * contexts) == 0 and contexts == 1 + len(EARLY) + len(LATE)
        if paired and cores == 2 and mesh.shape["groups"] == 2:
            return split_by_heads(contexts, cores, *arrays)
        return split_by_context(*arrays)

    return jax.shard_map(
        local,
        mesh=mesh,
        in_specs=(
            P(("groups", "ctx"), "tp", None),
            P(("groups", "ctx"), None),
            P("ctx", "tp", None),
            P("groups"),
            P("groups"),
        ),
        out_specs=P(("groups", "ctx"), "tp", None),
        check_vma=False,
    )
```
